256 devices in a mesh: pair: 2 (over y_lo), narrow: 8 (over x, y_hi), wide: 16 (over z, core).
Axes of the slice: x: 4, y: 4 (y_hi: 2, y_lo: 2; y = y_hi * 2 + y_lo), z: 8, core: 2. Of those that a mesh axis runs over, the one named last changes fastest.
Arguments:
- frame_one: bfloat16 [98304, 128], P(('pair', 'narrow', 'wide')), parts along dimension 0, may hold values from -8 to 8
- frame_two: bfloat16 [98304, 128], P(('pair', 'wide', 'narrow')), parts along dimension 0, may hold values from -8 to 8
Outputs:
- flow_forward: float32 [2, 98304], P(None, ('pair', 'narrow', 'wide')), parts along dimension 1
- flow_backward: float32 [2, 98304], P(None, ('pair', 'wide', 'narrow')), parts along dimension 1
The draws below stay inside these ranges and needn't reach their ends.
There are 2 independent parts, one for each index of `pair`. The reference program is written for one: setup_inputs(seed, part) draws one part's arguments, and reference() takes and returns one part's arrays. A program takes and returns all parts, laid end to end along the dimension named above; each array names one. Nothing has to cross between parts.
All inputs are finite; a program needn't handle non-finite values.
Results may differ from the reference program's by a relative error of at most 0.0003.
Values may be sent and summed in bfloat16 or wider, within the bound.
No kernel may reach another device: no remote copies, remote signals or barrier semaphores. Data moves between devices by JAX's collectives and lax.ppermute only.
A program may use at most 64 MiB of HBM per device.

```python
import math
import jax
import jax.numpy as jnp
from jax import lax

FEAT = 128
IMG_W = 384
PIX = 49152
IMG_H = 128


def sign_rows(background, key):
    pixel_index = jnp.arange(PIX, dtype=jnp.int32)
    spacing = PIX // 8
    region = pixel_index // spacing
    inside = pixel_index - region * spacing
    shift_range = max(spacing // 16, 1)
    offset = jax.random.randint(jax.random.fold_in(key, 13), (), 0, shift_range, dtype=jnp.int32) + 5 * spacing // 8
    chosen = (inside == offset) & ((region == 1) | (region == 4) | (region == 6))
    flips = jax.random.bernoulli(jax.random.fold_in(key, 11), 0.5, (PIX, FEAT))
    signs = jnp.where(flips, 8.0, -8.0).astype(jnp.float32)
    return jnp.where(chosen[:, None], signs, background)


def draw_frame_one(key, part):
    key = jax.random.fold_in(key, 5)
    background = 1.6 * jax.random.normal(key, (PIX, FEAT), jnp.float32)
    background = jnp.clip(background, -8.0, 8.0)
    return sign_rows(background, key).astype(jnp.bfloat16)


def draw_frame_two(key, part):
    key = jax.random.fold_in(key, 7)
    background = 1.6 * jax.random.normal(key, (PIX, FEAT), jnp.float32)
    background = jnp.clip(background, -8.0, 8.0)
    return sign_rows(background, key).astype(jnp.bfloat16)


def setup_inputs(seed: int = 0, part: int = 0) -> dict:
    splits = jax.random.split(jax.random.key(seed), 3)
    own_keys = jax.random.split(jax.random.fold_in(splits[2], part), 3)
    frame_one = draw_frame_one(jax.random.fold_in(jax.random.fold_in(splits[2], part), 71), part)
    frame_two = draw_frame_two(jax.random.fold_in(jax.random.fold_in(splits[2], part), 71), part)
    return {"frame_one": frame_one, "frame_two": frame_two}


def pixel_coords(first_pixel, count, img_w, img_h):
    pixel_index = first_pixel + jnp.arange(count, dtype=jnp.int32)
    across = (pixel_index % img_w).astype(jnp.float32) * (2.0 / (img_w - 1)) - 1.0
    downward = (pixel_index // img_w).astype(jnp.float32) * (2.0 / (img_h - 1)) - 1.0
    return (across, downward)

def soft_flow(queries, targets, target_x, target_y, score_scale):
    scores = jnp.dot(queries, targets.T, preferred_element_type=jnp.float32) * score_scale
    row_peak = lax.optimization_barrier(jnp.max(scores, axis=1))
    weights = jnp.exp(scores - row_peak[:, None])
    total = lax.optimization_barrier(jnp.sum(weights, axis=1))
    mean_x = lax.optimization_barrier(jnp.sum(weights * target_x[None, :], axis=1)) / total
    mean_y = lax.optimization_barrier(jnp.sum(weights * target_y[None, :], axis=1)) / total
    return jnp.stack([mean_x, mean_y])

def reference(frame_one, frame_two):
    score_scale = 1.0 / math.sqrt(FEAT)
    across, downward = pixel_coords(0, PIX, IMG_W, IMG_H)
    block_rows = math.gcd(PIX, 1024)

    def run_side(queries, targets):
        blocks = queries.reshape(PIX // block_rows, block_rows, FEAT)
        means = lax.map(lambda block: soft_flow(block, targets, across, downward, score_scale), blocks)
        means = jnp.transpose(means, (1, 0, 2)).reshape(2, PIX)
        return means - jnp.stack([across, downward])
    return (run_side(frame_one, frame_two), run_side(frame_two, frame_one))
```

```python
import functools
import math

import jax
import jax.numpy as jnp
from jax import lax
from jax.experimental import pallas as pl
from jax.experimental.pallas import tpu as pltpu
from jax.sharding import PartitionSpec as P

IMG_W = 384
LANES = 128
THIRDS = IMG_W // LANES
STRIPS = IMG_W // 8
LOWEST = -3.0e38
HIGH = 2.0**100
LOW = 2.0**-80
f32 = jnp.float32
bf16 = jnp.bfloat16
VMEM = pl.BlockSpec(memory_space=pltpu.VMEM)
SMEM = pl.BlockSpec(memory_space=pltpu.SMEM)


def matmul_nt(left, right):
    return lax.dot_general(left, right, (((1,), (1,)), ((), ())), preferred_element_type=f32)


def merged(first, second):
    peak = jnp.maximum(first[0:1], second[0:1])
    sums = first * jnp.exp2(first[0:1] - peak) + second * jnp.exp2(second[0:1] - peak)
    row = lax.broadcasted_iota(jnp.int32, first.shape, 0)
    return jnp.where(row == 0, peak, sums)


def match_kernel(n_rows, n_cols, scale, place, u_ref, v_ref, rows_ref, cols_ref,
                 u2, v2, score, part, flush, peaks, n_col, x_col, y_col, slow_row, slow_col, flags):
    span = n_cols * LANES
    wide = THIRDS * span
    half = n_cols // 2

    def v_order(b):
        return lax.rem(b + place[2] * half, n_cols)

    for b in range(n_cols):
        start = pl.multiple_of(v_order(b) * IMG_W, IMG_W)
        for g in range(THIRDS):
            v2[g, b * LANES:(b + 1) * LANES, :] = v_ref[pl.ds(start + g * LANES, LANES), :]

    def split(a, carry):
        at = pl.ds(pl.multiple_of(a * IMG_W, IMG_W), IMG_W)
        scaled = u_ref[at, :].astype(f32) * scale
        top = scaled.astype(bf16)
        u2[at, :LANES] = top
        u2[at, LANES:] = (scaled - top.astype(f32)).astype(bf16)
        return carry

    lax.fori_loop(0, n_rows, split, 0)

    def clear():
        nothing = jnp.zeros((8, wide), f32)
        n_col[...] = nothing
        x_col[...] = nothing
        y_col[...] = nothing
        slow_col[...] = jnp.where(lax.broadcasted_iota(jnp.int32, (4, wide), 0) == 0, LOWEST, 0.0)

    clear()

    def clear_row():
        slow_row[...] = jnp.where(lax.broadcasted_iota(jnp.int32, (IMG_W, LANES), 1) == 0, LOWEST, 0.0)

    def fast(a, slot):
        left = u2[pl.ds(pl.multiple_of(a * IMG_W, IMG_W), IMG_W), :]
        for g in range(THIRDS):
            top = None
            for t in range(0, span, 512):
                right = v2[g, t:t + 512, :]
                s = matmul_nt(left, jnp.concatenate([right, right], axis=1))
                n = jnp.zeros((8, 512), f32)
                x = jnp.zeros((8, 512), f32)
                for h in range(STRIPS):
                    at = slice(8 * h, 8 * h + 8)
                    e = jnp.exp2(s[at, :])
                    n = n + e
                    x = x + n
                    piece = [e[:, k:k + LANES] for k in range(0, 512, LANES)]
                    if t:
                        run = part[slot, g, at, :LANES] + piece[0]
                        tot = part[slot, g, at, LANES:] + run
                    else:
                        run = piece[0]
                        tot = run
                    for p in piece[1:]:
                        run = run + p
                        tot = tot + run
                    part[slot, g, at, :LANES] = run
                    part[slot, g, at, LANES:] = tot
                flush[slot, g, 0, :, t:t + 512] = n
                flush[slot, g, 1, :, t:t + 512] = x
                m = jnp.maximum(jnp.maximum(n[:, :LANES], n[:, LANES:2 * LANES]),
                                jnp.maximum(n[:, 2 * LANES:3 * LANES], n[:, 3 * LANES:]))
                top = m if top is None else jnp.maximum(top, m)
            peaks[slot, g] = top

    lane = lax.broadcasted_iota(jnp.int32, (1, LANES), 1).astype(f32)
    sub4 = lax.broadcasted_iota(jnp.int32, (4, 3 * LANES), 0)
    third = lax.broadcasted_iota(jnp.int32, (4, 3 * LANES), 1) // LANES
    table = jnp.where(sub4 == third + 1, 1.0, 0.0).astype(bf16)
    table = jnp.concatenate([table, table], axis=1)

    def row_sums(slot):
        n = part[slot, 0, :, :LANES]
        x = n * lane
        y = part[slot, 0, :, LANES:]
        for g in range(1, THIRDS):
            more = part[slot, g, :, :LANES]
            n = n + more
            x = x + more * (lane + g * LANES)
            y = y + part[slot, g, :, LANES:]
        whole = jnp.concatenate([n, x, (place[3] + n_cols).astype(f32) * n - y], axis=1)
        top = whole.astype(bf16)
        rest = (whole - top.astype(f32)).astype(bf16)
        return matmul_nt(table, jnp.concatenate([top, rest], axis=1))

    def slow(a, g):
        left = u2[pl.ds(pl.multiple_of(a * IMG_W, IMG_W), IMG_W), :]
        offset = pl.multiple_of(g * span, span)

        def scores(t, carry):
            at = pl.ds(pl.multiple_of(t * 256, 256), 256)
            right = v2[g, at, :]
            score[:, at] = matmul_nt(left, jnp.concatenate([right, right], axis=1))
            return carry

        lax.fori_loop(0, span // 256, scores, 0)
        index = lax.broadcasted_iota(jnp.int32, (1, span), 1)
        down = (index // LANES + place[3]).astype(f32)
        across = (lax.rem(index, LANES) + g * LANES).astype(f32)
        column = lax.broadcasted_iota(jnp.int32, (64, LANES), 1)

        def by_row(h, peak):
            at = pl.ds(pl.multiple_of(h * 64, 64), 64)
            s = score[at, :]
            m = jnp.max(s, axis=1, keepdims=True)
            w = jnp.exp2(s - m)
            old = slow_row[at, :]
            new = jnp.where(column == 0, m, jnp.where(column == 1, jnp.sum(w, axis=1, keepdims=True), jnp.where(
                column == 2, jnp.sum(w * across, axis=1, keepdims=True), jnp.sum(w * down, axis=1, keepdims=True))))
            both = jnp.maximum(old[:, 0:1], m)
            sums = old * jnp.exp2(old[:, 0:1] - both) + new * jnp.exp2(m - both)
            slow_row[at, :] = jnp.where(column == 0, both, sums)
            for k in range(0, 64, 8):
                peak = jnp.maximum(peak, s[k:k + 8, :])
            return peak

        peak = lax.fori_loop(0, IMG_W // 64, by_row, jnp.full((8, span), LOWEST, f32))
        peak = jnp.max(peak, axis=0, keepdims=True)
        inner = lax.broadcasted_iota(jnp.int32, (8, 1), 0).astype(f32)

        def by_col(h, carry):
            n, x = carry
            for k in range(0, 32, 8):
                w = jnp.exp2(score[pl.ds(pl.multiple_of(h * 32 + k, 8), 8), :] - peak)
                n = n + w
                x = x + w * (inner + (h * 32 + k).astype(f32))
            return n, x

        nothing = jnp.zeros((8, span), f32)
        n, x = lax.fori_loop(0, IMG_W // 32, by_col, (nothing, nothing))
        n = jnp.sum(n, axis=0, keepdims=True)
        x = jnp.sum(x, axis=0, keepdims=True)
        row = lax.broadcasted_iota(jnp.int32, (4, span), 0)
        new = jnp.where(row == 0, peak, jnp.where(row == 1, n, jnp.where(row == 2, x, n * image_row(a))))
        at = pl.ds(offset, span)
        slow_col[:, at] = merged(slow_col[:, at], new)

    def image_row(a):
        return (place[0] + place[1] * a).astype(f32)

    def slow_stats():
        return jnp.transpose(slow_row[...])[0:4]

    def at_zero(stats):
        row = lax.broadcasted_iota(jnp.int32, stats.shape, 0)
        return jnp.where(row == 0, jnp.where(stats[1:2] > 0.0, 0.0, LOWEST), stats)

    def finish(a, slot, real):
        bad = [jnp.logical_not(jnp.max(peaks[slot, g]) < HIGH) for g in range(THIRDS)]
        for g in range(THIRDS):
            at = slice(g * span, (g + 1) * span)
            skip = jnp.logical_or(bad[g], jnp.logical_not(real))
            n = jnp.where(skip, 0.0, flush[slot, g, 0])
            x = jnp.where(skip, 0.0, flush[slot, g, 1])
            n_col[:, at] += n
            x_col[:, at] += x
            y_col[:, at] += n * image_row(a)
        rows_ref[a] = row_sums(slot)
        for g in range(THIRDS):
            flags[g] = bad[g].astype(jnp.int32)
        return jnp.logical_and(real, jnp.logical_or(jnp.logical_or(bad[0], bad[1]), bad[2]))

    def repair(a, slot):
        clear_row()

        def third_of(g, carry):
            @pl.when(flags[g] == 1)
            def _():
                part[slot, g] = jnp.zeros((IMG_W, 2 * LANES), f32)
                slow(a, g)
            return carry

        lax.fori_loop(0, THIRDS, third_of, 0)
        rows_ref[a] = merged(at_zero(row_sums(slot)), slow_stats())

    def body(a, carry):
        slot = lax.rem(a, 2)
        before = jnp.maximum(a - 1, 0)
        other = 1 - slot
        again = finish(before, other, a > 0)
        fast(a, slot)

        @pl.when(again)
        def _():
            repair(before, other)
        return carry

    lax.fori_loop(0, n_rows, body, 0)
    last = n_rows - 1
    again = finish(last, last % 2, last >= 0)

    @pl.when(again)
    def _():
        repair(last, last % 2)

    def columns():
        n = n_col[...]
        inner = lax.broadcasted_iota(jnp.int32, n.shape, 0).astype(f32)
        x = 8.0 * (STRIPS * n - x_col[...]) + n * inner
        row = lax.broadcasted_iota(jnp.int32, (4, wide), 0)
        sums = [jnp.sum(k, axis=0, keepdims=True) for k in (n, x, y_col[...])]
        fast_sums = jnp.where(row == 1, sums[0], jnp.where(row == 2, sums[1], jnp.where(row == 3, sums[2], 0.0)))
        return merged(at_zero(fast_sums), slow_col[...])

    def put(stats):
        for b in range(n_cols):
            to = v_order(b)
            for g in range(THIRDS):
                cols_ref[to, :, g * LANES:(g + 1) * LANES] = stats[:, g * span + b * LANES:g * span + (b + 1) * LANES]

    def least(stats):
        return jnp.min(stats[1:2] * jnp.exp2(stats[0:1]))

    stats = columns()
    put(stats)
    low = least(stats)
    rows_low = rows_ref[0][1:2] * jnp.exp2(rows_ref[0][0:1])
    for a in range(1, n_rows):
        rows_low = jnp.minimum(rows_low, rows_ref[a][1:2] * jnp.exp2(rows_ref[a][0:1]))
    low = jnp.minimum(low, jnp.min(rows_low))

    @pl.when(jnp.logical_not(low >= LOW))
    def _():
        clear()

        def whole_row(a, carry):
            clear_row()

            def one(g, inner):
                slow(a, g)
                return inner

            lax.fori_loop(0, THIRDS, one, 0)
            rows_ref[a] = slow_stats()
            return carry

        lax.fori_loop(0, n_rows, whole_row, 0)
        put(slow_col[...])


def match(place, u, v):
    n_rows, n_cols = u.shape[0] // IMG_W, v.shape[0] // IMG_W
    span = n_cols * LANES
    wide = THIRDS * span
    scale = math.log2(math.e) / math.sqrt(u.shape[1])
    return pl.pallas_call(
        functools.partial(match_kernel, n_rows, n_cols, scale),
        out_shape=(jax.ShapeDtypeStruct((n_rows, 4, IMG_W), f32), jax.ShapeDtypeStruct((n_cols, 4, IMG_W), f32)),
        in_specs=[SMEM, VMEM, VMEM],
        out_specs=(VMEM, VMEM),
        scratch_shapes=[
            pltpu.VMEM((n_rows * IMG_W, 2 * LANES), bf16),
            pltpu.VMEM((THIRDS, span, LANES), bf16),
            pltpu.VMEM((IMG_W, span), f32),
            pltpu.VMEM((2, THIRDS, IMG_W, 2 * LANES), f32),
            pltpu.VMEM((2, THIRDS, 2, 8, span), f32),
            pltpu.VMEM((2, THIRDS, 8, LANES), f32),
            pltpu.VMEM((8, wide), f32),
            pltpu.VMEM((8, wide), f32),
            pltpu.VMEM((8, wide), f32),
            pltpu.VMEM((IMG_W, LANES), f32),
            pltpu.VMEM((4, wide), f32),
            pltpu.SMEM((THIRDS,), jnp.int32),
        ],
        compiler_params=pltpu.CompilerParams(vmem_limit_bytes=56 * 1024 * 1024),
        name="match",
    )(place, u, v)


def merge_kernel(mine, theirs, out):
    for k in range(mine.shape[0]):
        out[k] = merged(mine[k], theirs[k])


def merge(mine, theirs):
    return pl.pallas_call(
        merge_kernel, out_shape=jax.ShapeDtypeStruct(mine.shape, f32), in_specs=[VMEM, VMEM], out_specs=VMEM, name="merge"
    )(mine, theirs)


def flow_kernel(place, one, two, forward, backward):
    across = lax.broadcasted_iota(jnp.int32, (1, IMG_W), 1).astype(f32)
    for k, (stats, out) in enumerate(((one, forward), (two, backward))):
        total = stats[0]
        for other in range(1, stats.shape[0]):
            total = merged(total, stats[other])
        down = place[k].astype(f32)
        out[0:1, :] = (total[2:3] / total[1:2] - across) * (2.0 / (IMG_W - 1))
        out[1:2, :] = (total[3:4] / total[1:2] - down) * (2.0 / (place[2].astype(f32) - 1.0))


def flow(place, one, two):
    out = jax.ShapeDtypeStruct((2, IMG_W), f32)
    return pl.pallas_call(
        flow_kernel, out_shape=(out, out), in_specs=[SMEM, VMEM, VMEM], out_specs=(VMEM, VMEM), name="flow"
    )(place, one, two)


def on_device(frame_one, frame_two):
    n_wide, n_narrow = lax.axis_size("wide"), lax.axis_size("narrow")
    n_z = n_wide // 2
    w, n = lax.axis_index("wide"), lax.axis_index("narrow")
    z, core = w // 2, w % 2
    along_z = [[2 * k + c for k in range(n_z)] for c in range(2)]
    flip = [(k, k ^ 1) for k in range(n_wide)]
    u = lax.all_gather(frame_one, "wide", axis=0, tiled=True, axis_index_groups=along_z)
    v = lax.all_gather(frame_two, "narrow", axis=0, tiled=True)
    v = jnp.concatenate([v, lax.ppermute(v, "wide", flip)], axis=0)
    own_one = n * n_wide + w
    own_two = w * n_narrow + n
    place = jnp.stack([n * n_wide + core, 2, core, 2 * z * n_narrow]).astype(jnp.int32)
    rows, cols = match(place, u, v)
    cols = merge(cols[:n_narrow], lax.ppermute(cols[n_narrow:], "wide", flip))
    rows = lax.all_to_all(rows, "wide", 0, 0, axis_index_groups=along_z)
    cols = lax.all_to_all(cols, "narrow", 0, 0)
    img_h = n_wide * n_narrow
    return flow(jnp.stack([own_one, own_two, img_h]).astype(jnp.int32), rows, cols)


def solution(mesh):
    placed = (P(("pair", "narrow", "wide"), None), P(("pair", "wide", "narrow"), None))
    return jax.shard_map(
        on_device,
        mesh=mesh,
        in_specs=placed,
        out_specs=(P(None, ("pair", "narrow", "wide")), P(None, ("pair", "wide", "narrow"))),
        check_vma=False,
    )
```

```python
import functools
import math

import jax
import jax.numpy as jnp
from jax import lax
from jax.experimental import pallas as pl
from jax.experimental.pallas import tpu as pltpu
from jax.sharding import PartitionSpec as P

IMG_W = 384
LANES = 128
THIRDS = IMG_W // LANES
STRIPS = IMG_W // 8
LOWEST = -3.0e38
HIGH = 2.0**100
LOW = 2.0**-80
f32 = jnp.float32
bf16 = jnp.bfloat16
VMEM = pl.BlockSpec(memory_space=pltpu.VMEM)
SMEM = pl.BlockSpec(memory_space=pltpu.SMEM)


def matmul_nt(left, right):
    return lax.dot_general(left, right, (((1,), (1,)), ((), ())), preferred_element_type=f32)


def merged(first, second):
    peak = jnp.maximum(first[0:1], second[0:1])
    sums = first * jnp.exp2(first[0:1] - peak) + second * jnp.exp2(second[0:1] - peak)
    row = lax.broadcasted_iota(jnp.int32, first.shape, 0)
    return jnp.where(row == 0, peak, sums)


def match_kernel(n_rows, n_cols, n_pieces, scale, place, u_ref, *refs):
    pieces, refs = refs[:n_pieces], refs[n_pieces:]
    (rows_ref, own_ref, other_ref, u2, v2, score, part, flush, peaks, n_col, x_col, y_col, slow_row, slow_col, flags) = refs
    span = n_cols * LANES
    wide = THIRDS * span
    half = n_cols // 2
    per_piece = n_cols // n_pieces

    for k in range(n_cols):
        piece, start = pieces[k // per_piece], k % per_piece * IMG_W
        to = pl.ds(pl.multiple_of(place[8 + k] * LANES, LANES), LANES)
        for g in range(THIRDS):
            v2[g, to, :] = piece[start + g * LANES:start + (g + 1) * LANES, :]

    def split(a, carry):
        at = pl.ds(pl.multiple_of(a * IMG_W, IMG_W), IMG_W)
        scaled = u_ref[at, :].astype(f32) * scale
        top = scaled.astype(bf16)
        u2[at, :LANES] = top
        u2[at, LANES:] = (scaled - top.astype(f32)).astype(bf16)
        return carry

    lax.fori_loop(0, n_rows, split, 0)

    def clear():
        nothing = jnp.zeros((8, wide), f32)
        n_col[...] = nothing
        x_col[...] = nothing
        y_col[...] = nothing
        slow_col[...] = jnp.where(lax.broadcasted_iota(jnp.int32, (4, wide), 0) == 0, LOWEST, 0.0)

    clear()

    def clear_row():
        slow_row[...] = jnp.where(lax.broadcasted_iota(jnp.int32, (IMG_W, LANES), 1) == 0, LOWEST, 0.0)

    def fast(a, slot):
        left = u2[pl.ds(pl.multiple_of(a * IMG_W, IMG_W), IMG_W), :]
        for g in range(THIRDS):
            top = None
            for t in range(0, span, 512):
                right = v2[g, t:t + 512, :]
                s = matmul_nt(left, jnp.concatenate([right, right], axis=1))
                n = jnp.zeros((8, 512), f32)
                x = jnp.zeros((8, 512), f32)
                for h in range(STRIPS):
                    at = slice(8 * h, 8 * h + 8)
                    e = jnp.exp2(s[at, :])
                    n = n + e
                    x = x + n
                    piece = [e[:, k:k + LANES] for k in range(0, 512, LANES)]
                    if t:
                        run = part[slot, g, at, :LANES] + piece[0]
                        tot = part[slot, g, at, LANES:] + run
                    else:
                        run = piece[0]
                        tot = run
                    for p in piece[1:]:
                        run = run + p
                        tot = tot + run
                    part[slot, g, at, :LANES] = run
                    part[slot, g, at, LANES:] = tot
                flush[slot, g, 0, :, t:t + 512] = n
                flush[slot, g, 1, :, t:t + 512] = x
                m = jnp.maximum(jnp.maximum(n[:, :LANES], n[:, LANES:2 * LANES]),
                                jnp.maximum(n[:, 2 * LANES:3 * LANES], n[:, 3 * LANES:]))
                top = m if top is None else jnp.maximum(top, m)
            peaks[slot, g] = top

    lane = lax.broadcasted_iota(jnp.int32, (1, LANES), 1).astype(f32)
    sub4 = lax.broadcasted_iota(jnp.int32, (4, 3 * LANES), 0)
    third = lax.broadcasted_iota(jnp.int32, (4, 3 * LANES), 1) // LANES
    table = jnp.where(sub4 == third + 1, 1.0, 0.0).astype(bf16)
    table = jnp.concatenate([table, table], axis=1)

    def row_sums(slot):
        n = part[slot, 0, :, :LANES]
        x = n * lane
        y = part[slot, 0, :, LANES:]
        for g in range(1, THIRDS):
            more = part[slot, g, :, :LANES]
            n = n + more
            x = x + more * (lane + g * LANES)
            y = y + part[slot, g, :, LANES:]
        whole = jnp.concatenate([n, x, (place[3] + n_cols).astype(f32) * n - y], axis=1)
        top = whole.astype(bf16)
        rest = (whole - top.astype(f32)).astype(bf16)
        return matmul_nt(table, jnp.concatenate([top, rest], axis=1))

    def slow(a, g):
        left = u2[pl.ds(pl.multiple_of(a * IMG_W, IMG_W), IMG_W), :]
        offset = pl.multiple_of(g * span, span)

        def scores(t, carry):
            at = pl.ds(pl.multiple_of(t * 256, 256), 256)
            right = v2[g, at, :]
            score[:, at] = matmul_nt(left, jnp.concatenate([right, right], axis=1))
            return carry

        lax.fori_loop(0, span // 256, scores, 0)
        index = lax.broadcasted_iota(jnp.int32, (1, span), 1)
        down = (index // LANES + place[3]).astype(f32)
        across = (lax.rem(index, LANES) + g * LANES).astype(f32)
        column = lax.broadcasted_iota(jnp.int32, (64, LANES), 1)

        def by_row(h, peak):
            at = pl.ds(pl.multiple_of(h * 64, 64), 64)
            s = score[at, :]
            m = jnp.max(s, axis=1, keepdims=True)
            w = jnp.exp2(s - m)
            old = slow_row[at, :]
            new = jnp.where(column == 0, m, jnp.where(column == 1, jnp.sum(w, axis=1, keepdims=True), jnp.where(
                column == 2, jnp.sum(w * across, axis=1, keepdims=True), jnp.sum(w * down, axis=1, keepdims=True))))
            both = jnp.maximum(old[:, 0:1], m)
            sums = old * jnp.exp2(old[:, 0:1] - both) + new * jnp.exp2(m - both)
            slow_row[at, :] = jnp.where(column == 0, both, sums)
            for k in range(0, 64, 8):
                peak = jnp.maximum(peak, s[k:k + 8, :])
            return peak

        peak = lax.fori_loop(0, IMG_W // 64, by_row, jnp.full((8, span), LOWEST, f32))
        peak = jnp.max(peak, axis=0, keepdims=True)
        inner = lax.broadcasted_iota(jnp.int32, (8, 1), 0).astype(f32)

        def by_col(h, carry):
            n, x = carry
            for k in range(0, 32, 8):
                w = jnp.exp2(score[pl.ds(pl.multiple_of(h * 32 + k, 8), 8), :] - peak)
                n = n + w
                x = x + w * (inner + (h * 32 + k).astype(f32))
            return n, x

        nothing = jnp.zeros((8, span), f32)
        n, x = lax.fori_loop(0, IMG_W // 32, by_col, (nothing, nothing))
        n = jnp.sum(n, axis=0, keepdims=True)
        x = jnp.sum(x, axis=0, keepdims=True)
        row = lax.broadcasted_iota(jnp.int32, (4, span), 0)
        new = jnp.where(row == 0, peak, jnp.where(row == 1, n, jnp.where(row == 2, x, n * image_row(a))))
        at = pl.ds(offset, span)
        slow_col[:, at] = merged(slow_col[:, at], new)

    def image_row(a):
        return (place[0] + place[1] * a).astype(f32)

    def slow_stats():
        return jnp.transpose(slow_row[...])[0:4]

    def at_zero(stats):
        row = lax.broadcasted_iota(jnp.int32, stats.shape, 0)
        return jnp.where(row == 0, jnp.where(stats[1:2] > 0.0, 0.0, LOWEST), stats)

    def finish(a, slot, real):
        bad = [jnp.logical_not(jnp.max(peaks[slot, g]) < HIGH) for g in range(THIRDS)]
        for g in range(THIRDS):
            at = slice(g * span, (g + 1) * span)
            skip = jnp.logical_or(bad[g], jnp.logical_not(real))
            n = jnp.where(skip, 0.0, flush[slot, g, 0])
            x = jnp.where(skip, 0.0, flush[slot, g, 1])
            n_col[:, at] += n
            x_col[:, at] += x
            y_col[:, at] += n * image_row(a)
        rows_ref[a] = row_sums(slot)
        for g in range(THIRDS):
            flags[g] = bad[g].astype(jnp.int32)
        return jnp.logical_and(real, jnp.logical_or(jnp.logical_or(bad[0], bad[1]), bad[2]))

    def repair(a, slot):
        clear_row()

        def third_of(g, carry):
            @pl.when(flags[g] == 1)
            def _():
                part[slot, g] = jnp.zeros((IMG_W, 2 * LANES), f32)
                slow(a, g)
            return carry

        lax.fori_loop(0, THIRDS, third_of, 0)
        rows_ref[a] = merged(at_zero(row_sums(slot)), slow_stats())

    def body(a, carry):
        slot = lax.rem(a, 2)
        before = jnp.maximum(a - 1, 0)
        other = 1 - slot
        again = finish(before, other, a > 0)
        fast(a, slot)

        @pl.when(again)
        def _():
            repair(before, other)
        return carry

    lax.fori_loop(0, n_rows, body, 0)
    last = n_rows - 1
    again = finish(last, last % 2, last >= 0)

    @pl.when(again)
    def _():
        repair(last, last % 2)

    def columns():
        n = n_col[...]
        inner = lax.broadcasted_iota(jnp.int32, n.shape, 0).astype(f32)
        x = 8.0 * (STRIPS * n - x_col[...]) + n * inner
        row = lax.broadcasted_iota(jnp.int32, (4, wide), 0)
        sums = [jnp.sum(k, axis=0, keepdims=True) for k in (n, x, y_col[...])]
        fast_sums = jnp.where(row == 1, sums[0], jnp.where(row == 2, sums[1], jnp.where(row == 3, sums[2], 0.0)))
        return merged(at_zero(fast_sums), slow_col[...])

    def put(stats):
        first = place[2] == 0
        for k in range(half):
            for g in range(THIRDS):
                low = stats[:, g * span + k * LANES:g * span + (k + 1) * LANES]
                high = stats[:, g * span + (k + half) * LANES:g * span + (k + half + 1) * LANES]
                own_ref[k, :, g * LANES:(g + 1) * LANES] = jnp.where(first, low, high)
                other_ref[k, :, g * LANES:(g + 1) * LANES] = jnp.where(first, high, low)

    def least(stats):
        return jnp.min(stats[1:2] * jnp.exp2(stats[0:1]))

    stats = columns()
    put(stats)
    low = least(stats)
    rows_low = rows_ref[0][1:2] * jnp.exp2(rows_ref[0][0:1])
    for a in range(1, n_rows):
        rows_low = jnp.minimum(rows_low, rows_ref[a][1:2] * jnp.exp2(rows_ref[a][0:1]))
    low = jnp.minimum(low, jnp.min(rows_low))

    @pl.when(jnp.logical_not(low >= LOW))
    def _():
        clear()

        def whole_row(a, carry):
            clear_row()

            def one(g, inner):
                slow(a, g)
                return inner

            lax.fori_loop(0, THIRDS, one, 0)
            rows_ref[a] = slow_stats()
            return carry

        lax.fori_loop(0, n_rows, whole_row, 0)
        put(slow_col[...])


def match(place, u, pieces):
    n_rows, n_cols = u.shape[0] // IMG_W, sum(p.shape[0] for p in pieces) // IMG_W
    out = jax.ShapeDtypeStruct((n_cols // 2, 4, IMG_W), f32)
    span = n_cols * LANES
    wide = THIRDS * span
    scale = math.log2(math.e) / math.sqrt(u.shape[1])
    return pl.pallas_call(
        functools.partial(match_kernel, n_rows, n_cols, len(pieces), scale),
        out_shape=(jax.ShapeDtypeStruct((n_rows, 4, IMG_W), f32), out, out),
        in_specs=[SMEM] + [VMEM] * (1 + len(pieces)),
        out_specs=(VMEM, VMEM, VMEM),
        scratch_shapes=[
            pltpu.VMEM((n_rows * IMG_W, 2 * LANES), bf16),
            pltpu.VMEM((THIRDS, span, LANES), bf16),
            pltpu.VMEM((IMG_W, span), f32),
            pltpu.VMEM((2, THIRDS, IMG_W, 2 * LANES), f32),
            pltpu.VMEM((2, THIRDS, 2, 8, span), f32),
            pltpu.VMEM((2, THIRDS, 8, LANES), f32),
            pltpu.VMEM((8, wide), f32),
            pltpu.VMEM((8, wide), f32),
            pltpu.VMEM((8, wide), f32),
            pltpu.VMEM((IMG_W, LANES), f32),
            pltpu.VMEM((4, wide), f32),
            pltpu.SMEM((THIRDS,), jnp.int32),
        ],
        compiler_params=pltpu.CompilerParams(vmem_limit_bytes=56 * 1024 * 1024),
        name="match",
    )(place, u, *pieces)


def merge_kernel(mine, theirs, out):
    for k in range(mine.shape[0]):
        out[k] = merged(mine[k], theirs[k])


def merge(mine, theirs):
    return pl.pallas_call(
        merge_kernel, out_shape=jax.ShapeDtypeStruct(mine.shape, f32), in_specs=[VMEM, VMEM], out_specs=VMEM, name="merge"
    )(mine, theirs)


def flow_kernel(place, one, two, forward, backward):
    across = lax.broadcasted_iota(jnp.int32, (1, IMG_W), 1).astype(f32)
    for k, (stats, out) in enumerate(((one, forward), (two, backward))):
        total = stats[0]
        for other in range(1, stats.shape[0]):
            total = merged(total, stats[other])
        down = place[4 + k].astype(f32)
        out[0:1, :] = (total[2:3] / total[1:2] - across) * (2.0 / (IMG_W - 1))
        out[1:2, :] = (total[3:4] / total[1:2] - down) * (2.0 / (place[6].astype(f32) - 1.0))


def flow(place, one, two):
    out = jax.ShapeDtypeStruct((2, IMG_W), f32)
    return pl.pallas_call(
        flow_kernel, out_shape=(out, out), in_specs=[SMEM, VMEM, VMEM], out_specs=(VMEM, VMEM), name="flow"
    )(place, one, two)


def on_device(frame_one, frame_two):
    n_wide, n_narrow = lax.axis_size("wide"), lax.axis_size("narrow")
    n_z, n_x = n_wide // 2, n_narrow // 2
    w, n = lax.axis_index("wide"), lax.axis_index("narrow")
    z, core = w >> 1, w & 1
    x, y = n >> 1, n & 1
    along_z = [[2 * k + c for k in range(n_z)] for c in range(2)]
    flip = [(k, k ^ 1) for k in range(n_wide)]
    hops = [0, 1, n_x - 1] + list(range(2, n_x - 1))

    def along_x(array, hop):
        return lax.ppermute(array, "narrow", [(k, (k + 2 * hop) % n_narrow) for k in range(n_narrow)])

    u = lax.all_to_all(jnp.broadcast_to(frame_one, (n_z,) + frame_one.shape), "wide", 0, 0, axis_index_groups=along_z)
    both = jnp.concatenate([frame_two, lax.ppermute(frame_two, "narrow", [(k, k ^ 1) for k in range(n_narrow)])])
    pieces = [both] + [along_x(both, hop) for hop in hops[1:]]
    pieces += [lax.ppermute(piece, "wide", flip) for piece in pieces]
    goes = [(core ^ c) * n_narrow + lax.rem(x + (n_x - hop), n_x) * 2 + (y ^ k) for c in range(2) for hop in hops for k in range(2)]
    own = [n * n_wide + w, w * n_narrow + n, n_wide * n_narrow, 0]
    place = jnp.stack([jnp.asarray(k, jnp.int32) for k in [n * n_wide + core, 2, core, 2 * z * n_narrow] + own + goes])
    rows, cols, other = match(place, u.reshape(-1, frame_one.shape[1]), pieces)
    cols = merge(cols, lax.ppermute(other, "wide", flip))
    rows = lax.all_to_all(rows, "wide", 0, 0, axis_index_groups=along_z)
    cols = lax.all_to_all(cols, "narrow", 0, 0)
    return flow(place, rows, cols)


def solution(mesh):
    placed = (P(("pair", "narrow", "wide"), None), P(("pair", "wide", "narrow"), None))
    return jax.shard_map(
        on_device,
        mesh=mesh,
        in_specs=placed,
        out_specs=(P(None, ("pair", "narrow", "wide")), P(None, ("pair", "wide", "narrow"))),
        check_vma=False,
    )
```

```python
import functools
import math

import jax
import jax.numpy as jnp
from jax import lax
from jax.experimental import pallas as pl
from jax.experimental.pallas import tpu as pltpu
from jax.sharding import PartitionSpec as P

IMG_W = 384
LANES = 128
THIRDS = IMG_W // LANES
STRIPS = IMG_W // 8
LOWEST = -3.0e38
HIGH = 2.0**100
LOW = 2.0**-80
f32 = jnp.float32
bf16 = jnp.bfloat16
VMEM = pl.BlockSpec(memory_space=pltpu.VMEM)
SMEM = pl.BlockSpec(memory_space=pltpu.SMEM)


def matmul_nt(left, right):
    return lax.dot_general(left, right, (((1,), (1,)), ((), ())), preferred_element_type=f32)


def merged(first, second):
    peak = jnp.maximum(first[0:1], second[0:1])
    sums = first * jnp.exp2(first[0:1] - peak) + second * jnp.exp2(second[0:1] - peak)
    row = lax.broadcasted_iota(jnp.int32, first.shape, 0)
    return jnp.where(row == 0, peak, sums)


def match_kernel(n_rows, n_cols, n_pieces, scale, place, u_ref, *refs):
    pieces, refs = refs[:n_pieces], refs[n_pieces:]
    n_hops = n_cols // 4
    rows_ref, hop_refs, refs = refs[0], refs[1:1 + n_hops], refs[1 + n_hops:]
    (by_col_ref, u2, v2, score, part, flush, peaks, n_col, x_col, y_col, slow_row, slow_col, flags) = refs
    span = n_cols * LANES
    wide = THIRDS * span
    per_piece = n_cols // n_pieces

    for k in range(n_cols):
        piece, start = pieces[k // per_piece], k % per_piece * IMG_W
        to = pl.ds(pl.multiple_of(place[8 + k] * LANES, LANES), LANES)
        for g in range(THIRDS):
            v2[g, to, :] = piece[start + g * LANES:start + (g + 1) * LANES, :]

    def split(a, carry):
        at = pl.ds(pl.multiple_of(a * IMG_W, IMG_W), IMG_W)
        scaled = u_ref[at, :].astype(f32) * scale
        top = scaled.astype(bf16)
        u2[at, :LANES] = top
        u2[at, LANES:] = (scaled - top.astype(f32)).astype(bf16)
        return carry

    lax.fori_loop(0, n_rows, split, 0)

    def clear():
        nothing = jnp.zeros((8, wide), f32)
        n_col[...] = nothing
        x_col[...] = nothing
        y_col[...] = nothing
        slow_col[...] = jnp.where(lax.broadcasted_iota(jnp.int32, (4, wide), 0) == 0, LOWEST, 0.0)

    clear()

    def clear_row():
        slow_row[...] = jnp.where(lax.broadcasted_iota(jnp.int32, (IMG_W, LANES), 1) == 0, LOWEST, 0.0)

    def fast(a, slot, thirds):
        left = u2[pl.ds(pl.multiple_of(a * IMG_W, IMG_W), IMG_W), :]
        for g in thirds:
            right = v2[g]
            s = matmul_nt(left, jnp.concatenate([right, right], axis=1))
            n = x = None
            for h in range(STRIPS):
                at = slice(8 * h, 8 * h + 8)
                e = jnp.exp2(s[at, :])
                n = n + e if h else e
                x = x + n if h else e
                run = tot = e[:, :LANES]
                for k in range(LANES, span, LANES):
                    run = run + e[:, k:k + LANES]
                    tot = tot + run
                part[slot, g, at, :LANES] = run
                part[slot, g, at, LANES:] = tot
            flush[slot, g, 0] = n
            flush[slot, g, 1] = x
            top = n[:, :LANES]
            for k in range(LANES, span, LANES):
                top = jnp.maximum(top, n[:, k:k + LANES])
            peaks[slot, g] = top

    lane = lax.broadcasted_iota(jnp.int32, (1, LANES), 1).astype(f32)
    sub4 = lax.broadcasted_iota(jnp.int32, (4, 3 * LANES), 0)
    third = lax.broadcasted_iota(jnp.int32, (4, 3 * LANES), 1) // LANES
    table = jnp.where(sub4 == third + 1, 1.0, 0.0).astype(bf16)
    table = jnp.concatenate([table, table], axis=1)

    def row_sums(slot):
        n = x = y = 0.0
        for g in range(THIRDS):
            total = part[slot, g, :, :LANES]
            n = n + total
            x = x + total * (lane + g * LANES)
            y = y + part[slot, g, :, LANES:]
        whole = jnp.concatenate([n, x, (place[3] + n_cols).astype(f32) * n - y], axis=1)
        top = whole.astype(bf16)
        rest = (whole - top.astype(f32)).astype(bf16)
        return matmul_nt(table, jnp.concatenate([top, rest], axis=1))

    def slow(a, g):
        left = u2[pl.ds(pl.multiple_of(a * IMG_W, IMG_W), IMG_W), :]
        offset = pl.multiple_of(g * span, span)

        def scores(t, carry):
            at = pl.ds(pl.multiple_of(t * 256, 256), 256)
            right = v2[g, at, :]
            score[:, at] = matmul_nt(left, jnp.concatenate([right, right], axis=1))
            return carry

        lax.fori_loop(0, span // 256, scores, 0)
        index = lax.broadcasted_iota(jnp.int32, (1, span), 1)
        down = (index // LANES + place[3]).astype(f32)
        across = (lax.rem(index, LANES) + g * LANES).astype(f32)
        column = lax.broadcasted_iota(jnp.int32, (64, LANES), 1)

        def by_row(h, peak):
            at = pl.ds(pl.multiple_of(h * 64, 64), 64)
            s = score[at, :]
            m = jnp.max(s, axis=1, keepdims=True)
            w = jnp.exp2(s - m)
            old = slow_row[at, :]
            new = jnp.where(column == 0, m, jnp.where(column == 1, jnp.sum(w, axis=1, keepdims=True), jnp.where(
                column == 2, jnp.sum(w * across, axis=1, keepdims=True), jnp.sum(w * down, axis=1, keepdims=True))))
            both = jnp.maximum(old[:, 0:1], m)
            sums = old * jnp.exp2(old[:, 0:1] - both) + new * jnp.exp2(m - both)
            slow_row[at, :] = jnp.where(column == 0, both, sums)
            for k in range(0, 64, 8):
                peak = jnp.maximum(peak, s[k:k + 8, :])
            return peak

        peak = lax.fori_loop(0, IMG_W // 64, by_row, jnp.full((8, span), LOWEST, f32))
        peak = jnp.max(peak, axis=0, keepdims=True)
        inner = lax.broadcasted_iota(jnp.int32, (8, 1), 0).astype(f32)

        def by_col(h, carry):
            n, x = carry
            for k in range(0, 32, 8):
                w = jnp.exp2(score[pl.ds(pl.multiple_of(h * 32 + k, 8), 8), :] - peak)
                n = n + w
                x = x + w * (inner + (h * 32 + k).astype(f32))
            return n, x

        nothing = jnp.zeros((8, span), f32)
        n, x = lax.fori_loop(0, IMG_W // 32, by_col, (nothing, nothing))
        n = jnp.sum(n, axis=0, keepdims=True)
        x = jnp.sum(x, axis=0, keepdims=True)
        row = lax.broadcasted_iota(jnp.int32, (4, span), 0)
        new = jnp.where(row == 0, peak, jnp.where(row == 1, n, jnp.where(row == 2, x, n * image_row(a))))
        at = pl.ds(offset, span)
        slow_col[:, at] = merged(slow_col[:, at], new)

    def image_row(a):
        return (place[0] + place[1] * a).astype(f32)

    def slow_stats():
        return jnp.transpose(slow_row[...])[0:4]

    def at_zero(stats):
        row = lax.broadcasted_iota(jnp.int32, stats.shape, 0)
        return jnp.where(row == 0, jnp.where(stats[1:2] > 0.0, 0.0, LOWEST), stats)

    def finish(a, slot, real):
        bad = [jnp.logical_not(jnp.max(peaks[slot, g]) < HIGH) for g in range(THIRDS)]
        for g in range(THIRDS):
            at = slice(g * span, (g + 1) * span)
            skip = jnp.logical_or(bad[g], jnp.logical_not(real))
            n = jnp.where(skip, 0.0, flush[slot, g, 0])
            x = jnp.where(skip, 0.0, flush[slot, g, 1])
            n_col[:, at] += n
            x_col[:, at] += x
            y_col[:, at] += n * image_row(a)
        rows_ref[a] = row_sums(slot)
        for g in range(THIRDS):
            flags[slot, g] = bad[g].astype(jnp.int32)
        return jnp.logical_and(real, jnp.logical_or(jnp.logical_or(bad[0], bad[1]), bad[2]))

    def repair(a, slot):
        clear_row()

        def third_of(g, carry):
            @pl.when(flags[slot, g] == 1)
            def _():
                part[slot, g] = jnp.zeros((IMG_W, 2 * LANES), f32)
                slow(a, g)
            return carry

        lax.fori_loop(0, THIRDS, third_of, 0)
        rows_ref[a] = merged(at_zero(row_sums(slot)), slow_stats())

    def two(i, carry):
        a = 2 * i
        slot = 2 * lax.rem(i, 2)
        before, was = jnp.maximum(a - 1, 0), 3 - slot
        again = finish(before, was, a > 0)
        fast(a, slot, range(THIRDS))
        fast(a + 1, slot + 1, range(1))
        again_too = finish(a, slot, a >= 0)
        fast(a + 1, slot + 1, range(1, THIRDS))

        @pl.when(again)
        def _():
            repair(before, was)

        @pl.when(again_too)
        def _():
            repair(a, slot)
        return carry

    lax.fori_loop(0, n_rows // 2, two, 0)
    last = n_rows - 1
    slot = 2 * ((n_rows // 2 - 1) % 2) + 1
    again = finish(last, slot, last >= 0)

    @pl.when(again)
    def _():
        repair(last, slot)

    def columns():
        n = n_col[...]
        inner = lax.broadcasted_iota(jnp.int32, n.shape, 0).astype(f32)
        x = 8.0 * (STRIPS * n - x_col[...]) + n * inner
        row = lax.broadcasted_iota(jnp.int32, (4, wide), 0)
        sums = [jnp.sum(k, axis=0, keepdims=True) for k in (n, x, y_col[...])]
        fast_sums = jnp.where(row == 1, sums[0], jnp.where(row == 2, sums[1], jnp.where(row == 3, sums[2], 0.0)))
        return merged(at_zero(fast_sums), slow_col[...])

    def put(stats):
        for b in range(n_cols):
            for g in range(THIRDS):
                by_col_ref[b, :, g * LANES:(g + 1) * LANES] = stats[:, g * span + b * LANES:g * span + (b + 1) * LANES]
        for k in range(n_cols):
            hop_refs[k // 4][k % 4 // 2, k % 2] = by_col_ref[place[8 + n_cols + k]]

    def least(stats):
        return jnp.min(stats[1:2] * jnp.exp2(stats[0:1]))

    stats = columns()
    put(stats)
    low = least(stats)
    rows_low = rows_ref[0][1:2] * jnp.exp2(rows_ref[0][0:1])
    for a in range(1, n_rows):
        rows_low = jnp.minimum(rows_low, rows_ref[a][1:2] * jnp.exp2(rows_ref[a][0:1]))
    low = jnp.minimum(low, jnp.min(rows_low))

    @pl.when(jnp.logical_not(low >= LOW))
    def _():
        clear()

        def whole_row(a, carry):
            clear_row()

            def one(g, inner):
                slow(a, g)
                return inner

            lax.fori_loop(0, THIRDS, one, 0)
            rows_ref[a] = slow_stats()
            return carry

        lax.fori_loop(0, n_rows, whole_row, 0)
        put(slow_col[...])


def match(place, u, pieces):
    n_rows, n_cols = u.shape[0] // IMG_W, sum(p.shape[0] for p in pieces) // IMG_W
    n_hops = n_cols // 4
    out = jax.ShapeDtypeStruct((2, 2, 4, IMG_W), f32)
    span = n_cols * LANES
    wide = THIRDS * span
    scale = math.log2(math.e) / math.sqrt(u.shape[1])
    return pl.pallas_call(
        functools.partial(match_kernel, n_rows, n_cols, len(pieces), scale),
        out_shape=(jax.ShapeDtypeStruct((n_rows, 4, IMG_W), f32),) + (out,) * n_hops,
        in_specs=[SMEM] + [VMEM] * (1 + len(pieces)),
        out_specs=(VMEM,) * (1 + n_hops),
        scratch_shapes=[
            pltpu.VMEM((n_cols, 4, IMG_W), f32),
            pltpu.VMEM((n_rows * IMG_W, 2 * LANES), bf16),
            pltpu.VMEM((THIRDS, span, LANES), bf16),
            pltpu.VMEM((IMG_W, span), f32),
            pltpu.VMEM((4, THIRDS, IMG_W, 2 * LANES), f32),
            pltpu.VMEM((4, THIRDS, 2, 8, span), f32),
            pltpu.VMEM((4, THIRDS, 8, LANES), f32),
            pltpu.VMEM((8, wide), f32),
            pltpu.VMEM((8, wide), f32),
            pltpu.VMEM((8, wide), f32),
            pltpu.VMEM((IMG_W, LANES), f32),
            pltpu.VMEM((4, wide), f32),
            pltpu.SMEM((4, THIRDS), jnp.int32),
        ],
        compiler_params=pltpu.CompilerParams(vmem_limit_bytes=56 * 1024 * 1024),
        name="match",
    )(place, u, *pieces)


def merged_parts(parts):
    peak = functools.reduce(jnp.maximum, [part[..., 0:1, :] for part in parts])
    sums = sum(part * jnp.exp2(part[..., 0:1, :] - peak) for part in parts)
    row = lax.broadcasted_iota(jnp.int32, sums.shape, sums.ndim - 2)
    return jnp.where(row == 0, peak, sums)


def flow_kernel(place, one, *refs):
    across = lax.broadcasted_iota(jnp.int32, (1, IMG_W), 1).astype(f32)
    first = one[0]
    for other in range(1, one.shape[0]):
        first = merged(first, one[other])
    mine, by_core, by_y, by_both, *outs = refs
    second = merged(merged(mine[...], by_core[...]), merged(by_y[0], by_both[1]))
    for k, (total, out) in enumerate(zip((first, second), outs)):
        down = place[4 + k].astype(f32)
        out[0:1, :] = (total[2:3] / total[1:2] - across) * (2.0 / (IMG_W - 1))
        out[1:2, :] = (total[3:4] / total[1:2] - down) * (2.0 / (place[6].astype(f32) - 1.0))


def flow(place, one, two):
    out = jax.ShapeDtypeStruct((2, IMG_W), f32)
    return pl.pallas_call(
        flow_kernel, out_shape=(out, out), in_specs=[SMEM] + [VMEM] * 5, out_specs=(VMEM, VMEM), name="flow"
    )(place, one, *two)


def on_device(frame_one, frame_two):
    n_wide, n_narrow = lax.axis_size("wide"), lax.axis_size("narrow")
    n_z, n_x = n_wide // 2, n_narrow // 2
    w, n = lax.axis_index("wide"), lax.axis_index("narrow")
    z, core = w >> 1, w & 1
    x, y = n >> 1, n & 1
    along_z = [[2 * k + c for k in range(n_z)] for c in range(2)]
    flip = [(k, k ^ 1) for k in range(n_wide)]
    flip_y = [(k, k ^ 1) for k in range(n_narrow)]
    hops = [0, 1, n_x - 1] + list(range(2, n_x - 1))

    def along_x(array, hop):
        return lax.ppermute(array, "narrow", [(k, (k + 2 * hop) % n_narrow) for k in range(n_narrow)])

    u = lax.all_to_all(jnp.broadcast_to(frame_one, (n_z,) + frame_one.shape), "wide", 0, 0, axis_index_groups=along_z)
    both = jnp.concatenate([frame_two, lax.ppermute(frame_two, "narrow", flip_y)])
    pieces = [both] + [along_x(both, hop) for hop in hops[1:]]
    pieces += [lax.ppermute(piece, "wide", flip) for piece in pieces]
    goes = [(core ^ c) * n_narrow + lax.rem(x + (n_x - hop), n_x) * 2 + (y ^ k) for c in range(2) for hop in hops for k in range(2)]
    sends = [(core ^ c) * n_narrow + lax.rem(x + hop, n_x) * 2 + (y ^ k) for hop in range(n_x) for c in range(2) for k in range(2)]
    own = [n * n_wide + w, w * n_narrow + n, n_wide * n_narrow, 0]
    place = jnp.stack([jnp.asarray(k, jnp.int32) for k in [n * n_wide + core, 2, core, 2 * z * n_narrow] + own + goes + sends])
    rows, *parts = match(place, u.reshape(-1, frame_one.shape[1]), pieces)
    rows = lax.all_to_all(rows, "wide", 0, 0, axis_index_groups=along_z)
    parts = [parts[0]] + [along_x(parts[hop], hop) for hop in hops[1:]]
    by_y = lax.ppermute(merged_parts([part[:, 1] for part in parts]), "narrow", flip_y)
    mine = merged_parts([part[0, 0] for part in parts])
    by_core = lax.ppermute(merged_parts([part[1, 0] for part in parts]), "wide", flip)
    by_both = lax.ppermute(by_y, "wide", flip)
    return flow(place, rows, [mine, by_core, by_y, by_both])


def solution(mesh):
    placed = (P(("pair", "narrow", "wide"), None), P(("pair", "wide", "narrow"), None))
    return jax.shard_map(
        on_device,
        mesh=mesh,
        in_specs=placed,
        out_specs=(P(None, ("pair", "narrow", "wide")), P(None, ("pair", "wide", "narrow"))),
        check_vma=False,
    )
```

```python
import functools
import math

import jax
import jax.numpy as jnp
from jax import lax
from jax.experimental import pallas as pl
from jax.experimental.pallas import tpu as pltpu
from jax.sharding import PartitionSpec as P

IMG_W = 384
LANES = 128
THIRDS = IMG_W // LANES
STRIPS = IMG_W // 8
LOWEST = -3.0e38
HIGH = 2.0**100
LOW = 2.0**-80
f32 = jnp.float32
bf16 = jnp.bfloat16
VMEM = pl.BlockSpec(memory_space=pltpu.VMEM)
SMEM = pl.BlockSpec(memory_space=pltpu.SMEM)


def matmul_nt(left, right):
    return lax.dot_general(left, right, (((1,), (1,)), ((), ())), preferred_element_type=f32)


def merged(first, second):
    peak = jnp.maximum(first[0:1], second[0:1])
    sums = first * jnp.exp2(first[0:1] - peak) + second * jnp.exp2(second[0:1] - peak)
    row = lax.broadcasted_iota(jnp.int32, first.shape, 0)
    return jnp.where(row == 0, peak, sums)


def match_kernel(n_rows, n_cols, n_pieces, scale, place, u_ref, *refs):
    pieces, refs = refs[:n_pieces], refs[n_pieces:]
    n_hops = n_cols // 4
    rows_ref, hop_refs, refs = refs[0], refs[1:1 + n_hops], refs[1 + n_hops:]
    (by_col_ref, u2, v2, score, part, flush, peaks, n_col, x_col, y_col, slow_row, slow_col, flags) = refs
    span = n_cols * LANES
    wide = THIRDS * span
    per_piece = n_cols // n_pieces

    for k in range(n_cols):
        piece, start = pieces[k // per_piece], k % per_piece * IMG_W
        to = pl.ds(pl.multiple_of(place[8 + k] * LANES, LANES), LANES)
        for g in range(THIRDS):
            v2[g, to, :] = piece[start + g * LANES:start + (g + 1) * LANES, :]

    def split(a, carry):
        at = pl.ds(pl.multiple_of(a * IMG_W, IMG_W), IMG_W)
        scaled = u_ref[at, :].astype(f32) * scale
        top = scaled.astype(bf16)
        u2[at, :LANES] = top
        u2[at, LANES:] = (scaled - top.astype(f32)).astype(bf16)
        return carry

    lax.fori_loop(0, n_rows, split, 0)

    def clear():
        nothing = jnp.zeros((8, wide), f32)
        n_col[...] = nothing
        x_col[...] = nothing
        y_col[...] = nothing
        slow_col[...] = jnp.where(lax.broadcasted_iota(jnp.int32, (4, wide), 0) == 0, LOWEST, 0.0)

    clear()

    def clear_row():
        slow_row[...] = jnp.where(lax.broadcasted_iota(jnp.int32, (IMG_W, LANES), 1) == 0, LOWEST, 0.0)

    def fast(a, slot, thirds):
        left = u2[pl.ds(pl.multiple_of(a * IMG_W, IMG_W), IMG_W), :]
        for g in thirds:
            right = v2[g]
            s = matmul_nt(left, jnp.concatenate([right, right], axis=1))
            n = x = None
            for h in range(STRIPS):
                at = slice(8 * h, 8 * h + 8)
                e = jnp.exp2(s[at, :])
                n = n + e if h else e
                x = x + n if h else e
                run = tot = e[:, :LANES]
                for k in range(LANES, span, LANES):
                    run = run + e[:, k:k + LANES]
                    tot = tot + run
                part[slot, g, at, :LANES] = run
                part[slot, g, at, LANES:] = tot
            flush[slot, g, 0] = n
            flush[slot, g, 1] = x
            top = n[:, :LANES]
            for k in range(LANES, span, LANES):
                top = jnp.maximum(top, n[:, k:k + LANES])
            peaks[slot, g] = top

    kind = lax.broadcasted_iota(jnp.int32, (4, 3 * LANES), 0)
    column = lax.broadcasted_iota(jnp.int32, (4, 3 * LANES), 1)
    first, second = column < LANES, column < 2 * LANES
    table = jnp.where(kind == 1, jnp.where(first, 1, 0), jnp.where(
        kind == 2, jnp.where(first, column, jnp.where(second, LANES, 0)), jnp.where(second, 0, kind // 3)))
    table = table.astype(bf16)
    table = jnp.concatenate([table, table], axis=1)

    def row_sums(slot):
        n = [part[slot, g, :, :LANES] for g in range(THIRDS)]
        y = [part[slot, g, :, LANES:] for g in range(THIRDS)]
        upper = n[1] + n[2]
        whole = jnp.concatenate([n[0] + upper, upper + n[2], y[0] + y[1] + y[2]], axis=1)
        top = whole.astype(bf16)
        rest = (whole - top.astype(f32)).astype(bf16)
        sums = matmul_nt(table, jnp.concatenate([top, rest], axis=1))
        row = lax.broadcasted_iota(jnp.int32, sums.shape, 0)
        return jnp.where(row == 3, (place[3] + n_cols).astype(f32) * sums[1:2] - sums, sums)

    def slow(a, g):
        left = u2[pl.ds(pl.multiple_of(a * IMG_W, IMG_W), IMG_W), :]
        offset = pl.multiple_of(g * span, span)

        def scores(t, carry):
            at = pl.ds(pl.multiple_of(t * 256, 256), 256)
            right = v2[g, at, :]
            score[:, at] = matmul_nt(left, jnp.concatenate([right, right], axis=1))
            return carry

        lax.fori_loop(0, span // 256, scores, 0)
        index = lax.broadcasted_iota(jnp.int32, (1, span), 1)
        down = (index // LANES + place[3]).astype(f32)
        across = (lax.rem(index, LANES) + g * LANES).astype(f32)
        column = lax.broadcasted_iota(jnp.int32, (64, LANES), 1)

        def by_row(h, peak):
            at = pl.ds(pl.multiple_of(h * 64, 64), 64)
            s = score[at, :]
            m = jnp.max(s, axis=1, keepdims=True)
            w = jnp.exp2(s - m)
            old = slow_row[at, :]
            new = jnp.where(column == 0, m, jnp.where(column == 1, jnp.sum(w, axis=1, keepdims=True), jnp.where(
                column == 2, jnp.sum(w * across, axis=1, keepdims=True), jnp.sum(w * down, axis=1, keepdims=True))))
            both = jnp.maximum(old[:, 0:1], m)
            sums = old * jnp.exp2(old[:, 0:1] - both) + new * jnp.exp2(m - both)
            slow_row[at, :] = jnp.where(column == 0, both, sums)
            for k in range(0, 64, 8):
                peak = jnp.maximum(peak, s[k:k + 8, :])
            return peak

        peak = lax.fori_loop(0, IMG_W // 64, by_row, jnp.full((8, span), LOWEST, f32))
        peak = jnp.max(peak, axis=0, keepdims=True)
        inner = lax.broadcasted_iota(jnp.int32, (8, 1), 0).astype(f32)

        def by_col(h, carry):
            n, x = carry
            for k in range(0, 32, 8):
                w = jnp.exp2(score[pl.ds(pl.multiple_of(h * 32 + k, 8), 8), :] - peak)
                n = n + w
                x = x + w * (inner + (h * 32 + k).astype(f32))
            return n, x

        nothing = jnp.zeros((8, span), f32)
        n, x = lax.fori_loop(0, IMG_W // 32, by_col, (nothing, nothing))
        n = jnp.sum(n, axis=0, keepdims=True)
        x = jnp.sum(x, axis=0, keepdims=True)
        row = lax.broadcasted_iota(jnp.int32, (4, span), 0)
        new = jnp.where(row == 0, peak, jnp.where(row == 1, n, jnp.where(row == 2, x, n * image_row(a))))
        at = pl.ds(offset, span)
        slow_col[:, at] = merged(slow_col[:, at], new)

    def image_row(a):
        return (place[0] + place[1] * a).astype(f32)

    def slow_stats():
        return jnp.transpose(slow_row[...])[0:4]

    def at_zero(stats):
        row = lax.broadcasted_iota(jnp.int32, stats.shape, 0)
        return jnp.where(row == 0, jnp.where(stats[1:2] > 0.0, 0.0, LOWEST), stats)

    def finish(a, slot, real):
        bad = [jnp.logical_not(jnp.max(peaks[slot, g]) < HIGH) for g in range(THIRDS)]
        for g in range(THIRDS):
            at = slice(g * span, (g + 1) * span)
            skip = jnp.logical_or(bad[g], jnp.logical_not(real))
            n = jnp.where(skip, 0.0, flush[slot, g, 0])
            x = jnp.where(skip, 0.0, flush[slot, g, 1])
            n_col[:, at] += n
            x_col[:, at] += x
            y_col[:, at] += n * image_row(a)
        rows_ref[a] = row_sums(slot)
        for g in range(THIRDS):
            flags[slot, g] = bad[g].astype(jnp.int32)
        return jnp.logical_and(real, jnp.logical_or(jnp.logical_or(bad[0], bad[1]), bad[2]))

    def repair(a, slot):
        clear_row()

        def third_of(g, carry):
            @pl.when(flags[slot, g] == 1)
            def _():
                part[slot, g] = jnp.zeros((IMG_W, 2 * LANES), f32)
                slow(a, g)
            return carry

        lax.fori_loop(0, THIRDS, third_of, 0)
        rows_ref[a] = merged(at_zero(row_sums(slot)), slow_stats())

    def two(i, carry):
        a = 2 * i
        slot = 2 * lax.rem(i, 2)
        before, was = jnp.maximum(a - 1, 0), 3 - slot
        again = finish(before, was, a > 0)
        fast(a, slot, range(THIRDS))
        fast(a + 1, slot + 1, range(1))
        again_too = finish(a, slot, a >= 0)
        fast(a + 1, slot + 1, range(1, THIRDS))

        @pl.when(again)
        def _():
            repair(before, was)

        @pl.when(again_too)
        def _():
            repair(a, slot)
        return carry

    lax.fori_loop(0, n_rows // 2, two, 0)
    last = n_rows - 1
    slot = 2 * ((n_rows // 2 - 1) % 2) + 1
    again = finish(last, slot, last >= 0)

    @pl.when(again)
    def _():
        repair(last, slot)

    def columns():
        n = n_col[...]
        inner = lax.broadcasted_iota(jnp.int32, n.shape, 0).astype(f32)
        x = 8.0 * (STRIPS * n - x_col[...]) + n * inner
        row = lax.broadcasted_iota(jnp.int32, (4, wide), 0)
        sums = [jnp.sum(k, axis=0, keepdims=True) for k in (n, x, y_col[...])]
        fast_sums = jnp.where(row == 1, sums[0], jnp.where(row == 2, sums[1], jnp.where(row == 3, sums[2], 0.0)))
        return merged(at_zero(fast_sums), slow_col[...])

    def put(stats):
        for b in range(n_cols):
            for g in range(THIRDS):
                by_col_ref[b, :, g * LANES:(g + 1) * LANES] = stats[:, g * span + b * LANES:g * span + (b + 1) * LANES]
        for k in range(n_cols):
            hop_refs[k // 4][k % 4 // 2, k % 2] = by_col_ref[place[8 + n_cols + k]]

    def least(stats):
        return jnp.min(stats[1:2] * jnp.exp2(stats[0:1]))

    stats = columns()
    put(stats)
    low = least(stats)
    rows_low = rows_ref[0][1:2] * jnp.exp2(rows_ref[0][0:1])
    for a in range(1, n_rows):
        rows_low = jnp.minimum(rows_low, rows_ref[a][1:2] * jnp.exp2(rows_ref[a][0:1]))
    low = jnp.minimum(low, jnp.min(rows_low))

    @pl.when(jnp.logical_not(low >= LOW))
    def _():
        clear()

        def whole_row(a, carry):
            clear_row()

            def one(g, inner):
                slow(a, g)
                return inner

            lax.fori_loop(0, THIRDS, one, 0)
            rows_ref[a] = slow_stats()
            return carry

        lax.fori_loop(0, n_rows, whole_row, 0)
        put(slow_col[...])


def match(place, u, pieces):
    n_rows, n_cols = u.shape[0] // IMG_W, sum(p.shape[0] for p in pieces) // IMG_W
    n_hops = n_cols // 4
    out = jax.ShapeDtypeStruct((2, 2, 4, IMG_W), f32)
    span = n_cols * LANES
    wide = THIRDS * span
    scale = math.log2(math.e) / math.sqrt(u.shape[1])
    return pl.pallas_call(
        functools.partial(match_kernel, n_rows, n_cols, len(pieces), scale),
        out_shape=(jax.ShapeDtypeStruct((n_rows, 4, IMG_W), f32),) + (out,) * n_hops,
        in_specs=[SMEM] + [VMEM] * (1 + len(pieces)),
        out_specs=(VMEM,) * (1 + n_hops),
        scratch_shapes=[
            pltpu.VMEM((n_cols, 4, IMG_W), f32),
            pltpu.VMEM((n_rows * IMG_W, 2 * LANES), bf16),
            pltpu.VMEM((THIRDS, span, LANES), bf16),
            pltpu.VMEM((IMG_W, span), f32),
            pltpu.VMEM((4, THIRDS, IMG_W, 2 * LANES), f32),
            pltpu.VMEM((4, THIRDS, 2, 8, span), f32),
            pltpu.VMEM((4, THIRDS, 8, LANES), f32),
            pltpu.VMEM((8, wide), f32),
            pltpu.VMEM((8, wide), f32),
            pltpu.VMEM((8, wide), f32),
            pltpu.VMEM((IMG_W, LANES), f32),
            pltpu.VMEM((4, wide), f32),
            pltpu.SMEM((4, THIRDS), jnp.int32),
        ],
        compiler_params=pltpu.CompilerParams(vmem_limit_bytes=56 * 1024 * 1024),
        name="match",
    )(place, u, *pieces)


def merged_parts(parts):
    peak = functools.reduce(jnp.maximum, [part[..., 0:1, :] for part in parts])
    sums = sum(part * jnp.exp2(part[..., 0:1, :] - peak) for part in parts)
    row = lax.broadcasted_iota(jnp.int32, sums.shape, sums.ndim - 2)
    return jnp.where(row == 0, peak, sums)


def flow_kernel(place, one, *refs):
    across = lax.broadcasted_iota(jnp.int32, (1, IMG_W), 1).astype(f32)
    first = one[0]
    for other in range(1, one.shape[0]):
        first = merged(first, one[other])
    mine, by_core, by_y, by_both, *outs = refs
    second = merged(merged(mine[...], by_core[...]), merged(by_y[0], by_both[1]))
    for k, (total, out) in enumerate(zip((first, second), outs)):
        down = place[4 + k].astype(f32)
        out[0:1, :] = (total[2:3] / total[1:2] - across) * (2.0 / (IMG_W - 1))
        out[1:2, :] = (total[3:4] / total[1:2] - down) * (2.0 / (place[6].astype(f32) - 1.0))


def flow(place, one, two):
    out = jax.ShapeDtypeStruct((2, IMG_W), f32)
    return pl.pallas_call(
        flow_kernel, out_shape=(out, out), in_specs=[SMEM] + [VMEM] * 5, out_specs=(VMEM, VMEM), name="flow"
    )(place, one, *two)


def on_device(frame_one, frame_two):
    n_wide, n_narrow = lax.axis_size("wide"), lax.axis_size("narrow")
    n_z, n_x = n_wide // 2, n_narrow // 2
    w, n = lax.axis_index("wide"), lax.axis_index("narrow")
    z, core = w >> 1, w & 1
    x, y = n >> 1, n & 1
    along_z = [[2 * k for k in range(n_z)], [2 * k + 1 for k in reversed(range(n_z))]]
    flip = [(k, k ^ 1) for k in range(n_wide)]
    flip_y = [(k, k ^ 1) for k in range(n_narrow)]
    hops = [0, 1, n_x - 1] + list(range(2, n_x - 1))

    def along_x(array, hop):
        return lax.ppermute(array, "narrow", [(k, (k + 2 * hop) % n_narrow) for k in range(n_narrow)])

    u = lax.all_to_all(jnp.broadcast_to(frame_one, (n_z,) + frame_one.shape), "wide", 0, 0, axis_index_groups=along_z)
    both = jnp.concatenate([frame_two, lax.ppermute(frame_two, "narrow", flip_y)])
    pieces = [both] + [along_x(both, hop) for hop in hops[1:]]
    pieces += [lax.ppermute(piece, "wide", flip) for piece in pieces]
    goes = [(core ^ c) * n_narrow + lax.rem(x + (n_x - hop), n_x) * 2 + (y ^ k) for c in range(2) for hop in hops for k in range(2)]
    sends = [(core ^ c) * n_narrow + lax.rem(x + hop, n_x) * 2 + (y ^ k) for hop in range(n_x) for c in range(2) for k in range(2)]
    own = [n * n_wide + w, w * n_narrow + n, n_wide * n_narrow, 0]
    place = jnp.stack([jnp.asarray(k, jnp.int32) for k in [n * n_wide + core + core * 2 * (n_z - 1), 2 - 4 * core, core, 2 * z * n_narrow] + own + goes + sends])
    rows, *parts = match(place, u.reshape(-1, frame_one.shape[1]), pieces)
    rows = lax.all_to_all(rows, "wide", 0, 0, axis_index_groups=along_z)
    parts = [parts[0]] + [along_x(parts[hop], hop) for hop in hops[1:]]
    by_y = lax.ppermute(merged_parts([part[:, 1] for part in parts]), "narrow", flip_y)
    mine = merged_parts([part[0, 0] for part in parts])
    by_core = lax.ppermute(merged_parts([part[1, 0] for part in parts]), "wide", flip)
    by_both = lax.ppermute(by_y, "wide", flip)
    return flow(place, rows, [mine, by_core, by_y, by_both])


def solution(mesh):
    placed = (P(("pair", "narrow", "wide"), None), P(("pair", "wide", "narrow"), None))
    return jax.shard_map(
        on_device,
        mesh=mesh,
        in_specs=placed,
        out_specs=(P(None, ("pair", "narrow", "wide")), P(None, ("pair", "wide", "narrow"))),
        check_vma=False,
    )
```

```python
import functools
import math

import jax
import jax.numpy as jnp
from jax import lax
from jax.experimental import pallas as pl
from jax.experimental.pallas import tpu as pltpu
from jax.sharding import PartitionSpec as P

IMG_W = 384
LANES = 128
THIRDS = IMG_W // LANES
STRIPS = IMG_W // 8
LOWEST = -3.0e38
HIGH = 2.0**100
LOW = 2.0**-80
f32 = jnp.float32
bf16 = jnp.bfloat16
VMEM = pl.BlockSpec(memory_space=pltpu.VMEM)
SMEM = pl.BlockSpec(memory_space=pltpu.SMEM)


def matmul_nt(left, right):
    return lax.dot_general(left, right, (((1,), (1,)), ((), ())), preferred_element_type=f32)


def merged(first, second):
    peak = jnp.maximum(first[0:1], second[0:1])
    sums = first * jnp.exp2(first[0:1] - peak) + second * jnp.exp2(second[0:1] - peak)
    row = lax.broadcasted_iota(jnp.int32, first.shape, 0)
    return jnp.where(row == 0, peak, sums)


def match_kernel(n_rows, n_cols, n_pieces, scale, place, u_ref, *refs):
    pieces, refs = refs[:n_pieces], refs[n_pieces:]
    n_hops = n_cols // 4
    rows_ref, hop_refs, refs = refs[0], refs[1:1 + n_hops], refs[1 + n_hops:]
    (by_col_ref, u2, v2, score, part, flush, peaks, n_col, x_col, y_col, slow_row, slow_col, flags) = refs
    span = n_cols * LANES
    wide = THIRDS * span
    per_piece = n_cols // n_pieces

    for k in range(n_cols):
        piece, start = pieces[k // per_piece], k % per_piece * IMG_W
        to = pl.ds(pl.multiple_of(place[8 + k] * LANES, LANES), LANES)
        for g in range(THIRDS):
            v2[g, to, :] = piece[start + g * LANES:start + (g + 1) * LANES, :]

    def split(a, carry):
        at = pl.ds(pl.multiple_of(a * IMG_W, IMG_W), IMG_W)
        scaled = u_ref[at, :].astype(f32) * scale
        top = scaled.astype(bf16)
        u2[at, :LANES] = top
        u2[at, LANES:] = (scaled - top.astype(f32)).astype(bf16)
        return carry

    lax.fori_loop(0, n_rows, split, 0)

    def clear():
        nothing = jnp.zeros((8, wide), f32)
        n_col[...] = nothing
        x_col[...] = nothing
        y_col[...] = nothing
        slow_col[...] = jnp.where(lax.broadcasted_iota(jnp.int32, (4, wide), 0) == 0, LOWEST, 0.0)

    clear()

    def clear_row():
        slow_row[...] = jnp.where(lax.broadcasted_iota(jnp.int32, (IMG_W, LANES), 1) == 0, LOWEST, 0.0)

    def fast(a, slot, thirds):
        left = u2[pl.ds(pl.multiple_of(a * IMG_W, IMG_W), IMG_W), :]
        for g in thirds:
            right = v2[g]
            s = matmul_nt(left, jnp.concatenate([right, right], axis=1))
            n = x = None
            for h in range(STRIPS):
                at = slice(8 * h, 8 * h + 8)
                e = jnp.exp2(s[at, :])
                n = n + e if h else e
                x = x + n if h else e
                run = tot = e[:, :LANES]
                for k in range(LANES, span, LANES):
                    run = run + e[:, k:k + LANES]
                    tot = tot + run
                part[slot, g, at, :LANES] = run
                part[slot, g, at, LANES:] = tot
            flush[slot, g, 0] = n
            flush[slot, g, 1] = x
            top = n[:, :LANES]
            for k in range(LANES, span, LANES):
                top = jnp.maximum(top, n[:, k:k + LANES])
            peaks[slot, g] = top

    kind = lax.broadcasted_iota(jnp.int32, (4, 3 * LANES), 0)
    column = lax.broadcasted_iota(jnp.int32, (4, 3 * LANES), 1)
    first, second = column < LANES, column < 2 * LANES
    table = jnp.where(kind == 1, jnp.where(first, 1, 0), jnp.where(
        kind == 2, jnp.where(first, column, jnp.where(second, LANES, 0)), jnp.where(second, 0, kind // 3)))
    table = table.astype(bf16)
    table = jnp.concatenate([table, table], axis=1)

    def row_sums(slot):
        n = [part[slot, g, :, :LANES] for g in range(THIRDS)]
        y = [part[slot, g, :, LANES:] for g in range(THIRDS)]
        upper = n[1] + n[2]
        whole = jnp.concatenate([n[0] + upper, upper + n[2], y[0] + y[1] + y[2]], axis=1)
        top = whole.astype(bf16)
        rest = (whole - top.astype(f32)).astype(bf16)
        sums = matmul_nt(table, jnp.concatenate([top, rest], axis=1))
        row = lax.broadcasted_iota(jnp.int32, sums.shape, 0)
        return jnp.where(row == 3, (place[3] + n_cols).astype(f32) * sums[1:2] - sums, sums)

    def slow(a, g):
        left = u2[pl.ds(pl.multiple_of(a * IMG_W, IMG_W), IMG_W), :]
        offset = pl.multiple_of(g * span, span)

        right = v2[g]
        score[...] = matmul_nt(left, jnp.concatenate([right, right], axis=1))
        index = lax.broadcasted_iota(jnp.int32, (1, span), 1)
        down = (index // LANES + place[3]).astype(f32)
        across = (lax.rem(index, LANES) + g * LANES).astype(f32)
        column = lax.broadcasted_iota(jnp.int32, (8, LANES), 1)
        peak = None
        for h in range(STRIPS):
            at = slice(8 * h, 8 * h + 8)
            s = score[at, :]
            m = jnp.max(s, axis=1, keepdims=True)
            w = jnp.exp2(s - m)
            old = slow_row[at, :]
            new = jnp.where(column == 0, m, jnp.where(column == 1, jnp.sum(w, axis=1, keepdims=True), jnp.where(
                column == 2, jnp.sum(w * across, axis=1, keepdims=True), jnp.sum(w * down, axis=1, keepdims=True))))
            both = jnp.maximum(old[:, 0:1], m)
            sums = old * jnp.exp2(old[:, 0:1] - both) + new * jnp.exp2(m - both)
            slow_row[at, :] = jnp.where(column == 0, both, sums)
            peak = jnp.maximum(peak, s) if h else s
        peak = jnp.max(peak, axis=0, keepdims=True)
        n = x = None
        for h in range(STRIPS):
            w = jnp.exp2(score[8 * h:8 * h + 8, :] - peak)
            n = n + w if h else w
            x = x + n if h else w
        inner = lax.broadcasted_iota(jnp.int32, (8, 1), 0).astype(f32)
        x = 8.0 * (STRIPS * n - x) + n * inner
        n = jnp.sum(n, axis=0, keepdims=True)
        x = jnp.sum(x, axis=0, keepdims=True)
        row = lax.broadcasted_iota(jnp.int32, (4, span), 0)
        new = jnp.where(row == 0, peak, jnp.where(row == 1, n, jnp.where(row == 2, x, n * image_row(a))))
        at = pl.ds(offset, span)
        slow_col[:, at] = merged(slow_col[:, at], new)

    def image_row(a):
        return (place[0] + place[1] * a).astype(f32)

    def slow_stats():
        return jnp.transpose(slow_row[...])[0:4]

    def at_zero(stats):
        row = lax.broadcasted_iota(jnp.int32, stats.shape, 0)
        return jnp.where(row == 0, jnp.where(stats[1:2] > 0.0, 0.0, LOWEST), stats)

    def finish(a, slot, real):
        bad = [jnp.logical_not(jnp.max(peaks[slot, g]) < HIGH) for g in range(THIRDS)]
        for g in range(THIRDS):
            at = slice(g * span, (g + 1) * span)
            skip = jnp.logical_or(bad[g], jnp.logical_not(real))
            n = jnp.where(skip, 0.0, flush[slot, g, 0])
            x = jnp.where(skip, 0.0, flush[slot, g, 1])
            n_col[:, at] += n
            x_col[:, at] += x
            y_col[:, at] += n * image_row(a)
        rows_ref[a] = row_sums(slot)
        for g in range(THIRDS):
            flags[slot, g] = bad[g].astype(jnp.int32)
        return jnp.logical_and(real, jnp.logical_or(jnp.logical_or(bad[0], bad[1]), bad[2]))

    def repair(a, slot):
        clear_row()

        def third_of(g, carry):
            @pl.when(flags[slot, g] == 1)
            def _():
                part[slot, g] = jnp.zeros((IMG_W, 2 * LANES), f32)
                slow(a, g)
            return carry

        lax.fori_loop(0, THIRDS, third_of, 0)
        rows_ref[a] = merged(at_zero(row_sums(slot)), slow_stats())

    def two(i, carry):
        a = 2 * i
        slot = 2 * lax.rem(i, 2)
        before, was = jnp.maximum(a - 1, 0), 3 - slot
        again = finish(before, was, a > 0)
        fast(a, slot, range(THIRDS))
        fast(a + 1, slot + 1, range(1))
        again_too = finish(a, slot, a >= 0)
        fast(a + 1, slot + 1, range(1, THIRDS))

        @pl.when(jnp.logical_or(again, again_too))
        def _():
            def each(k, inner):
                @pl.when(jnp.where(k == 0, again, again_too))
                def _():
                    repair(jnp.where(k == 0, before, a), jnp.where(k == 0, was, slot))
                return inner

            lax.fori_loop(0, 2, each, 0)
        return carry

    lax.fori_loop(0, n_rows // 2, two, 0)
    last = n_rows - 1
    slot = 2 * ((n_rows // 2 - 1) % 2) + 1
    again = finish(last, slot, last >= 0)

    @pl.when(again)
    def _():
        repair(last, slot)

    def columns():
        n = n_col[...]
        inner = lax.broadcasted_iota(jnp.int32, n.shape, 0).astype(f32)
        x = 8.0 * (STRIPS * n - x_col[...]) + n * inner
        row = lax.broadcasted_iota(jnp.int32, (4, wide), 0)
        sums = [jnp.sum(k, axis=0, keepdims=True) for k in (n, x, y_col[...])]
        fast_sums = jnp.where(row == 1, sums[0], jnp.where(row == 2, sums[1], jnp.where(row == 3, sums[2], 0.0)))
        return merged(at_zero(fast_sums), slow_col[...])

    def put(stats):
        for b in range(n_cols):
            for g in range(THIRDS):
                by_col_ref[b, :, g * LANES:(g + 1) * LANES] = stats[:, g * span + b * LANES:g * span + (b + 1) * LANES]
        for k in range(n_cols):
            hop_refs[k // 4][k % 4 // 2, k % 2] = by_col_ref[place[8 + n_cols + k]]

    def least(stats):
        return jnp.min(stats[1:2] * jnp.exp2(stats[0:1]))

    stats = columns()
    put(stats)
    low = least(stats)
    rows_low = rows_ref[0][1:2] * jnp.exp2(rows_ref[0][0:1])
    for a in range(1, n_rows):
        rows_low = jnp.minimum(rows_low, rows_ref[a][1:2] * jnp.exp2(rows_ref[a][0:1]))
    low = jnp.minimum(low, jnp.min(rows_low))

    @pl.when(jnp.logical_not(low >= LOW))
    def _():
        clear()

        def whole_row(a, carry):
            clear_row()

            def one(g, inner):
                slow(a, g)
                return inner

            lax.fori_loop(0, THIRDS, one, 0)
            rows_ref[a] = slow_stats()
            return carry

        lax.fori_loop(0, n_rows, whole_row, 0)
        put(slow_col[...])


def match(place, u, pieces):
    n_rows, n_cols = u.shape[0] // IMG_W, sum(p.shape[0] for p in pieces) // IMG_W
    n_hops = n_cols // 4
    out = jax.ShapeDtypeStruct((2, 2, 4, IMG_W), f32)
    span = n_cols * LANES
    wide = THIRDS * span
    scale = math.log2(math.e) / math.sqrt(u.shape[1])
    return pl.pallas_call(
        functools.partial(match_kernel, n_rows, n_cols, len(pieces), scale),
        out_shape=(jax.ShapeDtypeStruct((n_rows, 4, IMG_W), f32),) + (out,) * n_hops,
        in_specs=[SMEM] + [VMEM] * (1 + len(pieces)),
        out_specs=(VMEM,) * (1 + n_hops),
        scratch_shapes=[
            pltpu.VMEM((n_cols, 4, IMG_W), f32),
            pltpu.VMEM((n_rows * IMG_W, 2 * LANES), bf16),
            pltpu.VMEM((THIRDS, span, LANES), bf16),
            pltpu.VMEM((IMG_W, span), f32),
            pltpu.VMEM((4, THIRDS, IMG_W, 2 * LANES), f32),
            pltpu.VMEM((4, THIRDS, 2, 8, span), f32),
            pltpu.VMEM((4, THIRDS, 8, LANES), f32),
            pltpu.VMEM((8, wide), f32),
            pltpu.VMEM((8, wide), f32),
            pltpu.VMEM((8, wide), f32),
            pltpu.VMEM((IMG_W, LANES), f32),
            pltpu.VMEM((4, wide), f32),
            pltpu.SMEM((4, THIRDS), jnp.int32),
        ],
        compiler_params=pltpu.CompilerParams(vmem_limit_bytes=56 * 1024 * 1024),
        name="match",
    )(place, u, *pieces)


def merged_parts(parts):
    peak = functools.reduce(jnp.maximum, [part[..., 0:1, :] for part in parts])
    sums = sum(part * jnp.exp2(part[..., 0:1, :] - peak) for part in parts)
    row = lax.broadcasted_iota(jnp.int32, sums.shape, sums.ndim - 2)
    return jnp.where(row == 0, peak, sums)


def flow_kernel(place, one, *refs):
    across = lax.broadcasted_iota(jnp.int32, (1, IMG_W), 1).astype(f32)
    first = one[0]
    for other in range(1, one.shape[0]):
        first = merged(first, one[other])
    mine, by_core, by_y, by_both, *outs = refs
    second = merged(merged(mine[...], by_core[...]), merged(by_y[0], by_both[1]))
    for k, (total, out) in enumerate(zip((first, second), outs)):
        down = place[4 + k].astype(f32)
        out[0:1, :] = (total[2:3] / total[1:2] - across) * (2.0 / (IMG_W - 1))
        out[1:2, :] = (total[3:4] / total[1:2] - down) * (2.0 / (place[6].astype(f32) - 1.0))


def flow(place, one, two):
    out = jax.ShapeDtypeStruct((2, IMG_W), f32)
    return pl.pallas_call(
        flow_kernel, out_shape=(out, out), in_specs=[SMEM] + [VMEM] * 5, out_specs=(VMEM, VMEM), name="flow"
    )(place, one, *two)


def on_device(frame_one, frame_two):
    n_wide, n_narrow = lax.axis_size("wide"), lax.axis_size("narrow")
    n_z, n_x = n_wide // 2, n_narrow // 2
    w, n = lax.axis_index("wide"), lax.axis_index("narrow")
    z, core = w >> 1, w & 1
    x, y = n >> 1, n & 1
    along_z = [[2 * k for k in range(n_z)], [2 * k + 1 for k in reversed(range(n_z))]]
    flip = [(k, k ^ 1) for k in range(n_wide)]
    flip_y = [(k, k ^ 1) for k in range(n_narrow)]
    hops = [0, 1, n_x - 1] + list(range(2, n_x - 1))

    def along_x(array, hop):
        return lax.ppermute(array, "narrow", [(k, (k + 2 * hop) % n_narrow) for k in range(n_narrow)])

    u = lax.all_to_all(jnp.broadcast_to(frame_one, (n_z,) + frame_one.shape), "wide", 0, 0, axis_index_groups=along_z)
    both = jnp.concatenate([frame_two, lax.ppermute(frame_two, "narrow", flip_y)])
    pieces = [both] + [along_x(both, hop) for hop in hops[1:]]
    pieces += [lax.ppermute(piece, "wide", flip) for piece in pieces]
    goes = [(core ^ c) * n_narrow + lax.rem(x + (n_x - hop), n_x) * 2 + (y ^ k) for c in range(2) for hop in hops for k in range(2)]
    sends = [(core ^ c) * n_narrow + lax.rem(x + hop, n_x) * 2 + (y ^ k) for hop in range(n_x) for c in range(2) for k in range(2)]
    own = [n * n_wide + w, w * n_narrow + n, n_wide * n_narrow, 0]
    place = jnp.stack([jnp.asarray(k, jnp.int32) for k in [n * n_wide + core + core * 2 * (n_z - 1), 2 - 4 * core, core, 2 * z * n_narrow] + own + goes + sends])
    rows, *parts = match(place, u.reshape(-1, frame_one.shape[1]), pieces)
    rows = lax.all_to_all(rows, "wide", 0, 0, axis_index_groups=along_z)
    parts = [parts[0]] + [along_x(parts[hop], hop) for hop in hops[1:]]
    by_y = lax.ppermute(merged_parts([part[:, 1] for part in parts]), "narrow", flip_y)
    mine = merged_parts([part[0, 0] for part in parts])
    by_core = lax.ppermute(merged_parts([part[1, 0] for part in parts]), "wide", flip)
    by_both = lax.ppermute(by_y, "wide", flip)
    return flow(place, rows, [mine, by_core, by_y, by_both])


def solution(mesh):
    placed = (P(("pair", "narrow", "wide"), None), P(("pair", "wide", "narrow"), None))
    return jax.shard_map(
        on_device,
        mesh=mesh,
        in_specs=placed,
        out_specs=(P(None, ("pair", "narrow", "wide")), P(None, ("pair", "wide", "narrow"))),
        check_vma=False,
    )
```

```python
import functools
import math

import jax
import jax.numpy as jnp
from jax import lax
from jax.experimental import pallas as pl
from jax.experimental.pallas import tpu as pltpu
from jax.sharding import PartitionSpec as P

IMG_W = 384
LANES = 128
THIRDS = IMG_W // LANES
STRIPS = IMG_W // 8
LOWEST = -3.0e38
HIGH = 2.0**100
LOW = 2.0**-80
f32 = jnp.float32
bf16 = jnp.bfloat16
VMEM = pl.BlockSpec(memory_space=pltpu.VMEM)
SMEM = pl.BlockSpec(memory_space=pltpu.SMEM)


def matmul_nt(left, right):
    return lax.dot_general(left, right, (((1,), (1,)), ((), ())), preferred_element_type=f32)


def merged(first, second):
    peak = jnp.maximum(first[0:1], second[0:1])
    sums = first * jnp.exp2(first[0:1] - peak) + second * jnp.exp2(second[0:1] - peak)
    row = lax.broadcasted_iota(jnp.int32, first.shape, 0)
    return jnp.where(row == 0, peak, sums)


def match_kernel(n_rows, n_cols, n_pieces, scale, place, u_ref, *refs):
    pieces, refs = refs[:n_pieces], refs[n_pieces:]
    n_hops = n_cols // 4
    rows_ref, hop_refs, refs = refs[0], refs[1:1 + n_hops], refs[1 + n_hops:]
    (by_col_ref, u2, v2, score, part, flush, peaks, n_col, x_col, y_col, slow_row, slow_col, flags) = refs
    span = n_cols * LANES
    wide = THIRDS * span
    per_piece = n_cols // n_pieces

    for k in range(n_cols):
        piece, start = pieces[k // per_piece], k % per_piece * IMG_W
        to = pl.ds(pl.multiple_of(place[8 + k] * LANES, LANES), LANES)
        for g in range(THIRDS):
            v2[g, to, :] = piece[start + g * LANES:start + (g + 1) * LANES, :]

    def split(a, carry):
        at = pl.ds(pl.multiple_of(a * IMG_W, IMG_W), IMG_W)
        scaled = u_ref[at, :].astype(f32) * scale
        top = scaled.astype(bf16)
        u2[at, :LANES] = top
        u2[at, LANES:] = (scaled - top.astype(f32)).astype(bf16)
        return carry

    lax.fori_loop(0, n_rows, split, 0)

    def clear():
        nothing = jnp.zeros((8, wide), f32)
        n_col[...] = nothing
        x_col[...] = nothing
        y_col[...] = nothing
        slow_col[...] = jnp.where(lax.broadcasted_iota(jnp.int32, (4, wide), 0) == 0, LOWEST, 0.0)

    clear()

    def clear_row():
        slow_row[...] = jnp.where(lax.broadcasted_iota(jnp.int32, (IMG_W, LANES), 1) == 0, LOWEST, 0.0)

    def fast(a, slot, thirds):
        left = u2[pl.ds(pl.multiple_of(a * IMG_W, IMG_W), IMG_W), :]
        for g in thirds:
            right = v2[g]
            s = matmul_nt(left, jnp.concatenate([right, right], axis=1))
            n = x = None
            for h in range(STRIPS):
                at = slice(8 * h, 8 * h + 8)
                e = jnp.exp2(s[at, :])
                n = n + e if h else e
                x = x + n if h else e
                run = tot = e[:, :LANES]
                for k in range(LANES, span, LANES):
                    run = run + e[:, k:k + LANES]
                    tot = tot + run
                part[slot, g, at, :LANES] = run
                part[slot, g, at, LANES:] = tot
            flush[slot, g, 0] = n
            flush[slot, g, 1] = x
            top = n[:, :LANES]
            for k in range(LANES, span, LANES):
                top = jnp.maximum(top, n[:, k:k + LANES])
            peaks[slot, g] = top

    kind = lax.broadcasted_iota(jnp.int32, (4, 3 * LANES), 0)
    column = lax.broadcasted_iota(jnp.int32, (4, 3 * LANES), 1)
    first, second = column < LANES, column < 2 * LANES
    table = jnp.where(kind == 1, jnp.where(first, 1, 0), jnp.where(
        kind == 2, jnp.where(first, column, jnp.where(second, LANES, 0)), jnp.where(second, 0, kind // 3)))
    table = table.astype(bf16)
    table = jnp.concatenate([table, table], axis=1)

    def row_sums(slot):
        n = [part[slot, g, :, :LANES] for g in range(THIRDS)]
        y = [part[slot, g, :, LANES:] for g in range(THIRDS)]
        upper = n[1] + n[2]
        whole = jnp.concatenate([n[0] + upper, upper + n[2], y[0] + y[1] + y[2]], axis=1)
        top = whole.astype(bf16)
        rest = (whole - top.astype(f32)).astype(bf16)
        sums = matmul_nt(table, jnp.concatenate([top, rest], axis=1))
        row = lax.broadcasted_iota(jnp.int32, sums.shape, 0)
        return jnp.where(row == 3, (place[3] + n_cols).astype(f32) * sums[1:2] - sums, sums)

    def slow(a, g):
        left = u2[pl.ds(pl.multiple_of(a * IMG_W, IMG_W), IMG_W), :]
        offset = pl.multiple_of(g * span, span)

        right = v2[g]
        score[...] = matmul_nt(left, jnp.concatenate([right, right], axis=1))
        index = lax.broadcasted_iota(jnp.int32, (1, span), 1)
        down = (index // LANES + place[3]).astype(f32)
        across = (lax.rem(index, LANES) + g * LANES).astype(f32)
        column = lax.broadcasted_iota(jnp.int32, (8, LANES), 1)
        peak = None
        for h in range(STRIPS):
            at = slice(8 * h, 8 * h + 8)
            s = score[at, :]
            m = jnp.max(s, axis=1, keepdims=True)
            w = jnp.exp2(s - m)
            old = slow_row[at, :]
            new = jnp.where(column == 0, m, jnp.where(column == 1, jnp.sum(w, axis=1, keepdims=True), jnp.where(
                column == 2, jnp.sum(w * across, axis=1, keepdims=True), jnp.sum(w * down, axis=1, keepdims=True))))
            both = jnp.maximum(old[:, 0:1], m)
            sums = old * jnp.exp2(old[:, 0:1] - both) + new * jnp.exp2(m - both)
            slow_row[at, :] = jnp.where(column == 0, both, sums)
            peak = jnp.maximum(peak, s) if h else s
        peak = jnp.max(peak, axis=0, keepdims=True)
        n = x = None
        for h in range(STRIPS):
            w = jnp.exp2(score[8 * h:8 * h + 8, :] - peak)
            n = n + w if h else w
            x = x + n if h else w
        inner = lax.broadcasted_iota(jnp.int32, (8, 1), 0).astype(f32)
        x = 8.0 * (STRIPS * n - x) + n * inner
        n = jnp.sum(n, axis=0, keepdims=True)
        x = jnp.sum(x, axis=0, keepdims=True)
        row = lax.broadcasted_iota(jnp.int32, (4, span), 0)
        new = jnp.where(row == 0, peak, jnp.where(row == 1, n, jnp.where(row == 2, x, n * image_row(a))))
        at = pl.ds(offset, span)
        slow_col[:, at] = merged(slow_col[:, at], new)

    def image_row(a):
        return (place[0] + place[1] * a).astype(f32)

    def slow_stats():
        return jnp.transpose(slow_row[...])[0:4]

    def at_zero(stats):
        row = lax.broadcasted_iota(jnp.int32, stats.shape, 0)
        return jnp.where(row == 0, jnp.where(stats[1:2] > 0.0, 0.0, LOWEST), stats)

    def finish(a, slot, real):
        bad = [jnp.logical_not(jnp.max(peaks[slot, g]) < HIGH) for g in range(THIRDS)]
        for g in range(THIRDS):
            at = slice(g * span, (g + 1) * span)
            skip = jnp.logical_or(bad[g], jnp.logical_not(real))
            n = jnp.where(skip, 0.0, flush[slot, g, 0])
            x = jnp.where(skip, 0.0, flush[slot, g, 1])
            n_col[:, at] += n
            x_col[:, at] += x
            y_col[:, at] += n * image_row(a)
        rows_ref[a] = row_sums(slot)
        for g in range(THIRDS):
            flags[slot, g] = bad[g].astype(jnp.int32)
        return jnp.logical_and(real, jnp.logical_or(jnp.logical_or(bad[0], bad[1]), bad[2]))

    def repair(a, slot):
        clear_row()

        def third_of(g, carry):
            @pl.when(flags[slot, g] == 1)
            def _():
                part[slot, g] = jnp.zeros((IMG_W, 2 * LANES), f32)
                slow(a, g)
            return carry

        lax.fori_loop(0, THIRDS, third_of, 0)
        rows_ref[a] = merged(at_zero(row_sums(slot)), slow_stats())

    def two(i, carry):
        a = 2 * i
        slot = 2 * lax.rem(i, 2)
        before, was = jnp.maximum(a - 1, 0), 3 - slot
        again = finish(before, was, a > 0)
        fast(a, slot, range(THIRDS))
        fast(a + 1, slot + 1, range(1))
        again_too = finish(a, slot, a >= 0)
        fast(a + 1, slot + 1, range(1, THIRDS))

        @pl.when(jnp.logical_or(again, again_too))
        def _():
            def each(k, inner):
                @pl.when(jnp.where(k == 0, again, again_too))
                def _():
                    repair(jnp.where(k == 0, before, a), jnp.where(k == 0, was, slot))
                return inner

            lax.fori_loop(0, 2, each, 0)
        return carry

    lax.fori_loop(0, n_rows // 2, two, 0)
    last = n_rows - 1
    slot = 2 * ((n_rows // 2 - 1) % 2) + 1
    again = finish(last, slot, last >= 0)

    @pl.when(again)
    def _():
        repair(last, slot)

    def columns():
        n = n_col[...]
        inner = lax.broadcasted_iota(jnp.int32, n.shape, 0).astype(f32)
        x = 8.0 * (STRIPS * n - x_col[...]) + n * inner
        row = lax.broadcasted_iota(jnp.int32, (4, wide), 0)
        sums = [jnp.sum(k, axis=0, keepdims=True) for k in (n, x, y_col[...])]
        fast_sums = jnp.where(row == 1, sums[0], jnp.where(row == 2, sums[1], jnp.where(row == 3, sums[2], 0.0)))
        return merged(at_zero(fast_sums), slow_col[...])

    def put(stats):
        for b in range(n_cols):
            for g in range(THIRDS):
                by_col_ref[b, :, g * LANES:(g + 1) * LANES] = stats[:, g * span + b * LANES:g * span + (b + 1) * LANES]
        for k in range(n_cols):
            hop_refs[k // 4][k % 4 // 2, k % 2] = by_col_ref[place[8 + n_cols + k]]

    def least(stats):
        return jnp.min(stats[1:2] * jnp.exp2(stats[0:1]))

    stats = columns()
    put(stats)
    low = least(stats)
    rows_low = rows_ref[0][1:2] * jnp.exp2(rows_ref[0][0:1])
    for a in range(1, n_rows):
        rows_low = jnp.minimum(rows_low, rows_ref[a][1:2] * jnp.exp2(rows_ref[a][0:1]))
    low = jnp.minimum(low, jnp.min(rows_low))

    @pl.when(jnp.logical_not(low >= LOW))
    def _():
        clear()

        def whole_row(a, carry):
            clear_row()

            def one(g, inner):
                slow(a, g)
                return inner

            lax.fori_loop(0, THIRDS, one, 0)
            rows_ref[a] = slow_stats()
            return carry

        lax.fori_loop(0, n_rows, whole_row, 0)
        put(slow_col[...])


def match(place, u, pieces):
    n_rows, n_cols = u.shape[0] // IMG_W, sum(p.shape[0] for p in pieces) // IMG_W
    n_hops = n_cols // 4
    out = jax.ShapeDtypeStruct((2, 2, 4, IMG_W), f32)
    span = n_cols * LANES
    wide = THIRDS * span
    scale = math.log2(math.e) / math.sqrt(u.shape[1])
    return pl.pallas_call(
        functools.partial(match_kernel, n_rows, n_cols, len(pieces), scale),
        out_shape=(jax.ShapeDtypeStruct((n_rows, 4, IMG_W), f32),) + (out,) * n_hops,
        in_specs=[SMEM] + [VMEM] * (1 + len(pieces)),
        out_specs=(VMEM,) * (1 + n_hops),
        scratch_shapes=[
            pltpu.VMEM((n_cols, 4, IMG_W), f32),
            pltpu.VMEM((n_rows * IMG_W, 2 * LANES), bf16),
            pltpu.VMEM((THIRDS, span, LANES), bf16),
            pltpu.VMEM((IMG_W, span), f32),
            pltpu.VMEM((4, THIRDS, IMG_W, 2 * LANES), f32),
            pltpu.VMEM((4, THIRDS, 2, 8, span), f32),
            pltpu.VMEM((4, THIRDS, 8, LANES), f32),
            pltpu.VMEM((8, wide), f32),
            pltpu.VMEM((8, wide), f32),
            pltpu.VMEM((8, wide), f32),
            pltpu.VMEM((IMG_W, LANES), f32),
            pltpu.VMEM((4, wide), f32),
            pltpu.SMEM((4, THIRDS), jnp.int32),
        ],
        compiler_params=pltpu.CompilerParams(vmem_limit_bytes=56 * 1024 * 1024),
        name="match",
    )(place, u, *pieces)


def merged_parts(parts):
    peak = functools.reduce(jnp.maximum, [part[..., 0:1, :] for part in parts])
    sums = sum(part * jnp.exp2(part[..., 0:1, :] - peak) for part in parts)
    row = lax.broadcasted_iota(jnp.int32, sums.shape, sums.ndim - 2)
    return jnp.where(row == 0, peak, sums)


def flow_kernel(place, one, *refs):
    across = lax.broadcasted_iota(jnp.int32, (1, IMG_W), 1).astype(f32)
    first = one[0]
    for other in range(1, one.shape[0]):
        first = merged(first, one[other])
    mine, by_core, by_y, by_both, *outs = refs
    second = merged(merged(mine[...], by_core[...]), merged(by_y[0], by_both[1]))
    for k, (total, out) in enumerate(zip((first, second), outs)):
        down = place[4 + k].astype(f32)
        out[0:1, :] = (total[2:3] / total[1:2] - across) * (2.0 / (IMG_W - 1))
        out[1:2, :] = (total[3:4] / total[1:2] - down) * (2.0 / (place[6].astype(f32) - 1.0))


def flow(place, one, two):
    out = jax.ShapeDtypeStruct((2, IMG_W), f32)
    return pl.pallas_call(
        flow_kernel, out_shape=(out, out), in_specs=[SMEM] + [VMEM] * 5, out_specs=(VMEM, VMEM), name="flow"
    )(place, one, *two)


def on_device(frame_one, frame_two):
    n_wide, n_narrow = lax.axis_size("wide"), lax.axis_size("narrow")
    n_z, n_x = n_wide // 2, n_narrow // 2
    w, n = lax.axis_index("wide"), lax.axis_index("narrow")
    z, core = w >> 1, w & 1
    x, y = n >> 1, n & 1
    along_z = [[2 * k for k in range(n_z)], [2 * k + 1 for k in reversed(range(n_z))]]
    flip = [(k, k ^ 1) for k in range(n_wide)]
    flip_y = [(k, k ^ 1) for k in range(n_narrow)]
    hops = [0, 1, n_x - 1] + list(range(2, n_x - 1))

    def along_x(array, hop):
        return lax.ppermute(array, "narrow", [(k, (k + 2 * hop) % n_narrow) for k in range(n_narrow)])

    u = lax.all_to_all(jnp.broadcast_to(frame_one, (n_z,) + frame_one.shape), "wide", 0, 0, axis_index_groups=along_z)
    both = jnp.concatenate([frame_two, lax.ppermute(frame_two, "narrow", flip_y)])
    pieces = [both] + [along_x(both, hop) for hop in hops[1:]]
    pieces += [lax.ppermute(piece, "wide", flip) for piece in pieces]
    goes = [(core ^ c) * n_narrow + lax.rem(x + (n_x - hop), n_x) * 2 + (y ^ k) for c in range(2) for hop in hops for k in range(2)]
    sends = [(core ^ c) * n_narrow + lax.rem(x + hop, n_x) * 2 + (y ^ k) for hop in range(n_x) for c in range(2) for k in range(2)]
    own = [n * n_wide + w, w * n_narrow + n, n_wide * n_narrow, 0]
    place = jnp.stack([jnp.asarray(k, jnp.int32) for k in [n * n_wide + core + core * 2 * (n_z - 1), 2 - 4 * core, core, 2 * z * n_narrow] + own + goes + sends])
    rows, *parts = match(place, u.reshape(-1, frame_one.shape[1]), pieces)
    rows = lax.all_to_all(rows, "wide", 0, 0, axis_index_groups=along_z)
    parts = [parts[0]] + [along_x(parts[hop], hop) for hop in hops[1:]]
    by_y = lax.ppermute(merged_parts([part[:, 1] for part in parts]), "narrow", flip_y)
    mine = merged_parts([part[0, 0] for part in parts])
    by_core = lax.ppermute(merged_parts([part[1, 0] for part in parts]), "wide", flip)
    rows, mine, by_core, by_y = lax.optimization_barrier((rows, mine, by_core, by_y))
    by_both = lax.ppermute(by_y, "wide", flip)
    return flow(place, rows, [mine, by_core, by_y, by_both])


def solution(mesh):
    placed = (P(("pair", "narrow", "wide"), None), P(("pair", "wide", "narrow"), None))
    return jax.shard_map(
        on_device,
        mesh=mesh,
        in_specs=placed,
        out_specs=(P(None, ("pair", "narrow", "wide")), P(None, ("pair", "wide", "narrow"))),
        check_vma=False,
    )
```
